128 devices in a mesh: batch: 2 (over core), member: 16 (over y, x), tensor: 4 (over z).
Axes of the slice: x: 4, y: 4, z: 4, core: 2. Of those that a mesh axis runs over, the one named last changes fastest.
Arguments:
- rows_in: bfloat16 [2048, 1536], P(('batch', 'member', 'tensor')), may hold values from -6 to 6
- target: bfloat16 [2048, 1536], P(('batch', 'member'), 'tensor'), may hold values from -6 to 6
- w_in: bfloat16 [16, 1536, 4096], P('member', None, 'tensor'), may hold values from -0.15309311 to 0.15309311, as said below
- w_out: bfloat16 [16, 4096, 1536], P('member', 'tensor'), may hold values from -0.09375 to 0.09375, as said below
Outputs:
- reward: float32 [2048], P(('batch', 'member', 'tensor'))
- grad_in: float32 [16, 1536, 4096], P('member', 'batch', 'tensor')
- grad_out: float32 [16, 4096, 1536], P('member', 'tensor', 'batch')
The draws below stay inside these ranges and needn't reach their ends.
Inputs may be any that keep to these rules, and one draw needn't show every extreme that they name: `w_in`: each entry lies within the stated bounds. `w_out`: each entry lies within the stated bounds.
All inputs are finite; a program needn't handle non-finite values.
Results may differ from the reference program's by a relative error of at most 0.0035.
The reference program's roundings to bfloat16 on the way (of `hidden`, `errors` and `pre_grad`) count: a program that leaves them out, or rounds other values in their place, can miss the bound.
Values may be sent and summed in bfloat16 or wider, within the bound.
A program may use at most 128 MiB of HBM per device.

```python
import jax
import jax.numpy as jnp
from jax import lax

F = 1536
H = 4096
ROWS = 2048
MEMBERS = 16


def draw_w_in(key, part):
    key = jax.random.fold_in(key, 11)
    common_key, member_key = jax.random.split(key)
    common = jax.random.normal(common_key, (1, F, H), jnp.float32)
    member_part = jax.random.normal(member_key, (MEMBERS, F, H), jnp.float32)
    mixed = 0.75 * common + 0.66 * member_part
    mixed = jnp.clip(mixed, -6.0, 6.0) * float(F) ** (-0.5)
    return mixed.astype(jnp.bfloat16)


def draw_w_out(key, part):
    key = jax.random.fold_in(key, 23)
    common_key, member_key = jax.random.split(key)
    common = jax.random.normal(common_key, (1, H, F), jnp.float32)
    member_part = jax.random.normal(member_key, (MEMBERS, H, F), jnp.float32)
    mixed = 0.75 * common + 0.66 * member_part
    mixed = jnp.clip(mixed, -6.0, 6.0) * float(H) ** (-0.5)
    return mixed.astype(jnp.bfloat16)


def level_of(key, dims, cuts, least, high):
    def one(dim, shards_of):
        draws = jax.random.uniform(jax.random.fold_in(jax.random.fold_in(key, 6), dim), (shards_of,), jnp.float32, least / len(cuts), high / len(cuts))
        return jnp.repeat(jnp.exp(draws), dims[dim] // shards_of).reshape((-1,) + (1,) * (len(dims) - dim - 1))

    loudness = one(*cuts[0])
    for cut in cuts[1:]:
        loudness = loudness * one(*cut)
    return loudness


def centred(key, dims, width, most, cuts=(), dtype=jnp.bfloat16):
    loudness = level_of(key, dims, cuts, -0.22, 0.18) if cuts else 1.0
    result = jax.random.normal(key, dims, jnp.float32) * width * loudness
    return jnp.minimum(jnp.maximum(result, -most), most).astype(dtype)


def setup_inputs(seed: int = 0) -> dict:
    arg_keys = jax.random.split(jax.random.key(seed), 5)
    return {
        "rows_in": centred(arg_keys[0], (ROWS, F), 1.0, 6.0, ((0, 128),)),
        "target": centred(arg_keys[1], (ROWS, F), 1.0, 6.0, ((0, 32), (1, 4))),
        "w_in": draw_w_in(jax.random.fold_in(arg_keys[4], 71), 0),
        "w_out": draw_w_out(jax.random.fold_in(arg_keys[4], 71), 0),
    }


def silu_slope(pre_act):
    sigmoid = jax.nn.sigmoid(pre_act)
    return sigmoid * (1.0 + pre_act * (1.0 - sigmoid))


def reference(rows_in, target, w_in, w_out):
    loss_scale = float(rows_in.shape[0]) ** -0.5
    target_wide = target.astype(jnp.float32)

    def one_member(weights):
        first_layer, second_layer = weights
        pre_act = jnp.dot(rows_in, first_layer, preferred_element_type=jnp.float32)
        hidden = jax.nn.silu(pre_act).astype(jnp.bfloat16)
        predicted = jnp.dot(hidden, second_layer, preferred_element_type=jnp.float32)
        errors = ((predicted - target_wide) * loss_scale).astype(jnp.bfloat16)
        grad_second = jnp.dot(hidden.T, errors, preferred_element_type=jnp.float32)
        back_grad = jnp.dot(errors, second_layer.T, preferred_element_type=jnp.float32)
        pre_grad = (back_grad * silu_slope(pre_act)).astype(jnp.bfloat16)
        grad_first = jnp.dot(rows_in.T, pre_grad, preferred_element_type=jnp.float32)
        return predicted, grad_first, grad_second

    predicted, grad_in, grad_out = lax.map(one_member, (w_in, w_out))
    member_mean = jnp.mean(predicted, axis=0)
    variance = jnp.mean((predicted - member_mean[None]) ** 2, axis=0)
    reward = jnp.mean(variance, axis=-1)
    return reward, grad_in, grad_out
```

```python
import jax
import jax.numpy as jnp
from jax import lax
from jax.experimental import pallas as pl
from jax.experimental.pallas import tpu as pltpu
from jax.sharding import PartitionSpec as P

MESH = pl.DeviceIdType.MESH
F32 = jnp.float32
BF16 = jnp.bfloat16

F = 1536
FH = F // 2
FQ = F // 4
HS = 1024
CH = 4
CR = 256
HALF = CR // 2
GR = CR // 4
W = F + FQ
MEMBERS = 16
SCALE = 2048.0**-0.5


def dot(a, b):
    return lax.dot_general(a, b, (((1,), (0,)), ((), ())), preferred_element_type=F32)


def dot_nt(a, b):
    return lax.dot_general(a, b, (((1,), (1,)), ((), ())), preferred_element_type=F32)


def dot_tn(a, b):
    return lax.dot_general(a, b, (((0,), (0,)), ((), ())), preferred_element_type=F32)


def kernel(
    rows_hbm, target_hbm, w_in_hbm, w_out_hbm,
    reward_ref, grad_in_hbm, grad_out_hbm,
    w_in, w_out, rows, rows_o, hid, slope, part, sbuf, rbuf, err, err_o, pre, acc_in, acc_out,
    pred_b, gathered, spread, spread_r,
    loc_sem, out_sem, zg_s, zg_r, p1_s, p1_r, p2_s, p2_r, rs_s, rs_r, ag_s, ag_r, core_s, core_r,
    rw_s, rw_r, rwl_sem, rz_s, rz_r,
):
    b = lax.axis_index("batch")
    m = lax.axis_index("member")
    t = lax.axis_index("tensor")
    y, x = m // 4, m % 4

    def z_dev(d):
        return (b, m, (t + d) % 4)

    def plane_dev(dy, dx):
        return (b, ((y + dy) % 4) * 4 + (x + dx) % 4, t)

    other = (1 - b, m, t)
    group_dev = [plane_dev(3, 0), plane_dev(1, 0), plane_dev(0, 3), plane_dev(0, 1)]

    def remote(src, dst, s, r, dev):
        return pltpu.make_async_remote_copy(
            src_ref=src, dst_ref=dst, send_sem=s, recv_sem=r, device_id=dev, device_id_type=MESH
        )

    def al(v, k):
        return pl.multiple_of(v, k)

    def quarter(q):
        return pl.ds(al((q % 4) * FQ, 128), FQ)

    mine_cols = pl.ds(al(b * FH, 128), FH)
    other_cols = pl.ds(al((1 - b) * FH, 128), FH)

    barrier = pltpu.get_barrier_semaphore()
    for d in range(1, 4):
        pl.semaphore_signal(barrier, inc=1, device_id=z_dev(d), device_id_type=MESH)
    pl.semaphore_signal(barrier, inc=1, device_id=other, device_id_type=MESH)

    @pl.loop(1, MEMBERS)
    def _(d):
        pl.semaphore_signal(
            barrier, inc=1, device_id=(b, (m + d) % MEMBERS, t), device_id_type=MESH
        )

    a_base = al(x * 32, 32)
    b_base = al(HALF + y * 32, 32)
    own_base = al(
        (1 - t // 2) * (x * 32 + t * 16) + (t // 2) * (HALF + y * 32 + (t - 2) * 16), 16
    )

    load_w_in = pltpu.make_async_copy(w_in_hbm.at[0], w_in, loc_sem.at[0])
    load_w_out = pltpu.make_async_copy(w_out_hbm.at[0], w_out, loc_sem.at[1])
    load_rows = pltpu.make_async_copy(
        rows_hbm, rows.at[0, pl.ds(own_base, 16), pl.ds(0, F)], loc_sem.at[2]
    )
    load_ta = pltpu.make_async_copy(
        target_hbm.at[pl.ds(0, 32)], rows.at[0, pl.ds(a_base, 32), pl.ds(F, FQ)], loc_sem.at[3]
    )
    load_tb = pltpu.make_async_copy(
        target_hbm.at[pl.ds(32, 32)], rows.at[0, pl.ds(b_base, 32), pl.ds(F, FQ)], loc_sem.at[4]
    )
    load_rows.start()
    load_ta.start()
    load_tb.start()

    pl.semaphore_wait(barrier, 3 + 1 + MEMBERS - 1)

    def z_gather(d):
        return remote(
            rows_hbm,
            rows.at[0, pl.ds(own_base, 16), pl.ds(0, F)],
            zg_s.at[d - 1],
            zg_r.at[d - 1],
            z_dev(d),
        )

    def z_gather_in(d):
        s = (t + 4 - d) % 4
        base = al((1 - s // 2) * (x * 32 + s * 16) + (s // 2) * (HALF + y * 32 + (s - 2) * 16), 16)
        return remote(
            rows_hbm,
            rows.at[0, pl.ds(base, 16), pl.ds(0, F)],
            zg_s.at[d - 1],
            zg_r.at[d - 1],
            z_dev(d),
        )

    for d in (2, 1, 3):
        z_gather(d).start()
    load_w_in.start()
    load_w_out.start()
    acc_in[...] = jnp.zeros_like(acc_in)
    acc_out[...] = jnp.zeros_like(acc_out)
    load_rows.wait()
    load_ta.wait()
    load_tb.wait()
    for d in (1, 3, 2):
        z_gather_in(d).wait_recv()

    def strip(axis, d):
        if axis == 0:
            return al(((x + d) % 4) * 32, 32)
        return al(HALF + ((y + d) % 4) * 32, 32)

    def axis_dev(axis, d):
        return plane_dev(0, d) if axis == 0 else plane_dev(d, 0)

    def phase1(axis, d):
        ref = rows.at[0, pl.ds(strip(axis, 0), 32)]
        k = axis * 4 + d // 2
        return remote(ref, ref, p1_s.at[k], p1_r.at[k], axis_dev(axis, d))

    def phase1_in(axis, d):
        ref = rows.at[0, pl.ds(strip(axis, 4 - d), 32)]
        k = axis * 4 + d // 2
        return remote(ref, ref, p1_s.at[k], p1_r.at[k], axis_dev(axis, d))

    def phase1_fwd(axis, d):
        ref = rows.at[0, pl.ds(al(strip(axis, 4 - d) + (d // 2) * 16, 16), 16)]
        k = axis * 4 + 2 + d // 2
        return remote(ref, ref, p1_s.at[k], p1_r.at[k], axis_dev(axis, d))

    def phase1_fwd_in(axis, d):
        ref = rows.at[0, pl.ds(al(strip(axis, 2) + (d // 2) * 16, 16), 16)]
        k = axis * 4 + 2 + d // 2
        return remote(ref, ref, p1_s.at[k], p1_r.at[k], axis_dev(axis, d))

    sides = [(0, 1), (0, 3), (1, 1), (1, 3)]
    for axis, d in sides:
        phase1(axis, d).start()
    for axis, d in sides:
        phase1_in(axis, d).wait_recv()
        phase1_fwd(axis, d).start()
    for axis, d in sides:
        phase1_fwd_in(axis, d).wait_recv()

    def phase2(c, g):
        src_chunk = 1 if c == 3 else 0
        src_group = g ^ 1 if c == 2 else g
        return remote(
            rows.at[src_chunk, pl.ds(src_group * GR, GR)],
            rows.at[c, pl.ds(g * GR, GR)],
            p2_s.at[c, g],
            p2_r.at[c, g],
            group_dev[g],
        )

    for c in (1, 2):
        for g in range(4):
            phase2(c, g).start()

    def core_copy(kind, c):
        src, dst = (
            (rows.at[c, :, other_cols], rows_o.at[c]),
            (hid.at[c, pl.ds(0, CR)], hid.at[c, pl.ds(CR, CR)]),
            (err.at[c, :, other_cols], err_o.at[c]),
            (pre.at[c, pl.ds(0, CR)], pre.at[c, pl.ds(CR, CR)]),
        )[kind]
        return remote(src, dst, core_s.at[kind, c], core_r.at[kind, c], other)

    def forward(c):
        core_copy(0, c).start()

        @pl.loop(0, HS // 256)
        def _(n):
            cols = pl.ds(al(n * 256, 256), 256)
            v = dot(rows[c, :, pl.ds(0, F)], w_in[:, cols])
            s = jax.nn.sigmoid(v)
            hid[c, pl.ds(0, CR), cols] = (v * s).astype(BF16)
            slope[c, :, cols] = s * (1.0 + v * (1.0 - s))

        core_copy(1, c).start()

        @pl.loop(0, 4)
        def _(k):
            rel = (3 + 2 * k - (k // 2)) % 4
            part[c, rel] = dot(hid[c, pl.ds(0, CR)], w_out[:, quarter(t + rel)])

            @pl.when(k == 0)
            def _():
                sbuf[c, 0, 0] = part[c, 3, pl.ds(0, HALF)].astype(BF16)
                rs(c, 0, 0).start()

            @pl.when(k == 1)
            def _():
                sbuf[c, 0, 1] = part[c, 1, pl.ds(HALF, HALF)].astype(BF16)
                rs(c, 0, 1).start()

    def rs(c, s, way):
        return remote(
            sbuf.at[c, s, way], rbuf.at[c, s, way], rs_s.at[c, s, way], rs_r.at[c, s, way],
            z_dev(1 if way == 0 else 3),
        )

    def rs_step(c, s):
        for way in range(2):
            rs(c, s - 1, way).wait_recv()
            rel = (3 - s) if way == 0 else (1 + s)
            own = part[c, rel, pl.ds(way * HALF, HALF)]
            sbuf[c, s, way] = (own + rbuf[c, s - 1, way].astype(F32)).astype(BF16)
            rs(c, s, way).start()

    def ag(c, way):
        ref = err.at[c, :, quarter(t)]
        return remote(ref, ref, ag_s.at[c, way], ag_r.at[c, way], z_dev(1 if way == 0 else 3))

    def ag_in(c, way):
        ref = err.at[c, :, quarter(t + (3 if way == 0 else 1))]
        return remote(ref, ref, ag_s.at[c, way], ag_r.at[c, way], z_dev(1 if way == 0 else 3))

    def ag_fwd(c, way):
        ref = err.at[c, pl.ds(way * HALF, HALF), quarter(t + (3 if way == 0 else 1))]
        k = 2 + way
        return remote(ref, ref, ag_s.at[c, k], ag_r.at[c, k], z_dev(1 if way == 0 else 3))

    def ag_fwd_in(c, way):
        ref = err.at[c, pl.ds(way * HALF, HALF), quarter(t + 2)]
        k = 2 + way
        return remote(ref, ref, ag_s.at[c, k], ag_r.at[c, k], z_dev(1 if way == 0 else 3))

    def reward_piece(c, p):
        first, second = (c + 1) // 2, (4 - (c + 1) // 2) % 4
        away = first if p % 4 < 2 else second
        idx = (p % 4 + 2 * ((c // 2) * (1 - c // 3))) % 4
        if p < 4:
            owner = ((y + away) % 4) * 4 + idx
        else:
            owner = idx * 4 + (x + away) % 4
        src = pred_b.at[c, pl.ds(32 * p, 32)]
        dst = gathered.at[m, pl.ds(32 * (p // 4), 32)]
        return owner, src, dst

    def reward_send(c):
        for p in range(8):
            owner, src, dst = reward_piece(c, p)

            @pl.when(owner != m)
            def _():
                remote(
                    src, dst, rw_s.at[c, p], rw_r.at[m, p // 4], (b, owner, t)
                ).start()

            @pl.when(owner == m)
            def _():
                pltpu.make_async_copy(src, dst, rwl_sem.at[p // 4]).start()

    def errors(c):
        for way in range(2):
            rs(c, 2, way).wait_recv()
            r = pl.ds(way * HALF, HALF)
            pred = part[c, 0, r] + rbuf[c, 2, way].astype(F32)
            goal = rows[c, r, pl.ds(F, FQ)].astype(F32)
            err[c, r, quarter(t)] = ((pred - goal) * SCALE).astype(BF16)
            pred_b[c, r] = pred.astype(BF16)
        ag(c, 0).start()
        ag(c, 1).start()
        reward_send(c)

    def ag_forward(c):
        for way in range(2):
            ag_in(c, way).wait_recv()
            ag_fwd(c, way).start()

    def back(c):
        for way in range(2):
            ag_fwd_in(c, way).wait_recv()
        core_copy(2, c).start()

        @pl.loop(0, HS // 256)
        def _(n):
            cols = pl.ds(al(n * 256, 256), 256)
            g = dot_nt(err[c], w_out[cols, :])
            pre[c, pl.ds(0, CR), cols] = (g * slope[c, :, cols]).astype(BF16)

        core_copy(3, c).start()

    def grads(c):
        core_copy(1, c).wait_recv()
        core_copy(2, c).wait_recv()

        @pl.loop(0, HS // 256)
        def _(n):
            cols = pl.ds(al(n * 256, 256), 256)
            acc_out[cols, :] += dot_tn(hid[c, pl.ds(0, CR), cols], err[c, :, mine_cols]) + dot_tn(
                hid[c, pl.ds(CR, CR), cols], err_o[c]
            )

        core_copy(0, c).wait_recv()
        core_copy(3, c).wait_recv()

        @pl.loop(0, FH // 256)
        def _(n):
            here = pl.ds(al(b * FH + n * 256, 128), 256)
            cols = pl.ds(al(n * 256, 256), 256)
            acc_in[cols, :] += dot_tn(rows[c, :, here], pre[c, pl.ds(0, CR)]) + dot_tn(
                rows_o[c, :, cols], pre[c, pl.ds(CR, CR)]
            )

    load_w_in.wait()
    load_w_out.wait()
    forward(0)

    def tick(i, carry):
        @pl.when(i >= 1)
        def _():
            errors(i - 1)

        @pl.when(i < CH)
        def _():
            rs_step(i, 1)

        @pl.when(i >= 2)
        def _():
            grads(i - 2)

        @pl.when(i >= 1)
        def _():
            ag_forward(i - 1)

        @pl.when(i < CH)
        def _():
            rs_step(i, 2)

        @pl.when(i < CH - 1)
        def _():
            for g in range(4):
                remote(
                    rows.at[0, pl.ds(0, GR)],
                    rows.at[i + 1, pl.ds(g * GR, GR)],
                    p2_s.at[i + 1, g],
                    p2_r.at[i + 1, g],
                    group_dev[g],
                ).wait_recv()

            @pl.when(i == 0)
            def _():
                for g in range(4):
                    phase2(3, g).start()

            forward(i + 1)

        @pl.when(i >= 1)
        def _():
            back(i - 1)

        return carry

    lax.fori_loop(0, CH + 1, tick, 0)

    def reward_in(s, half):
        return remote(
            pred_b.at[0, pl.ds(0, 32)],
            gathered.at[s, pl.ds(32 * half, 32)],
            rw_s.at[0, 0],
            rw_r.at[s, half],
            (b, s, t),
        )

    @pl.loop(0, MEMBERS)
    def _(s):
        @pl.when(s != m)
        def _():
            for half in range(2):
                reward_in(s, half).wait_recv()

        @pl.when(s == m)
        def _():
            for half in range(2):
                pltpu.make_async_copy(
                    pred_b.at[0, pl.ds(0, 32)],
                    gathered.at[s, pl.ds(32 * half, 32)],
                    rwl_sem.at[half],
                ).wait()

    total = jnp.zeros((64, 128), F32)
    for k in range(3):
        cols = pl.ds(128 * k, 128)
        mean = jnp.zeros((64, 128), F32)
        for s in range(MEMBERS):
            mean += gathered[s, :, cols].astype(F32)
        mean = mean * (1.0 / MEMBERS)
        for s in range(MEMBERS):
            dev = gathered[s, :, cols].astype(F32) - mean
            total += dev * dev
    spread[...] = total

    def spread_copy(d):
        return remote(
            spread.at[pl.ds(al(((t + d) % 4) * 16, 16), 16)],
            spread_r.at[d - 1],
            rz_s.at[d - 1],
            rz_r.at[d - 1],
            z_dev(d),
        )

    for d in range(1, 4):
        spread_copy(d).start()

    grads(CH - 1)
    out_in = pltpu.make_async_copy(acc_in, grad_in_hbm.at[0], out_sem.at[0])
    out_out = pltpu.make_async_copy(acc_out, grad_out_hbm.at[0], out_sem.at[1])
    out_in.start()
    out_out.start()

    for d in range(1, 4):
        spread_copy(d).wait_recv()
    own = spread[pl.ds(al(t * 16, 16), 16)]
    for d in range(3):
        own += spread_r[d]
    reward_ref[...] = jnp.sum(own, axis=1, keepdims=True) * (1.0 / (MEMBERS * F))

    for d in range(1, 4):
        z_gather(d).wait_send()
        spread_copy(d).wait_send()
    for axis, d in sides:
        phase1(axis, d).wait_send()
        phase1_fwd(axis, d).wait_send()
    for c in (1, 2, 3):
        for g in range(4):
            phase2(c, g).wait_send()

    @pl.loop(0, CH)
    def _(c):
        for way in range(2):
            for s in range(3):
                rs(c, s, way).wait_send()
            ag(c, way).wait_send()
            ag_fwd(c, way).wait_send()
        for kind in range(4):
            core_copy(kind, c).wait_send()
        for p in range(8):
            owner, src, dst = reward_piece(c, p)

            @pl.when(owner != m)
            def _():
                remote(src, dst, rw_s.at[c, p], rw_r.at[m, p // 4], (b, owner, t)).wait_send()

    out_in.wait()
    out_out.wait()


def per_device(rows_in, target, w_in, w_out):
    any_spec = pl.BlockSpec(memory_space=pl.ANY)
    vmem = pltpu.VMEM
    dma = pltpu.SemaphoreType.DMA
    reward, grad_in, grad_out = pl.pallas_call(
        kernel,
        out_shape=(
            jax.ShapeDtypeStruct((16, 1), F32),
            jax.ShapeDtypeStruct((1, FH, HS), F32),
            jax.ShapeDtypeStruct((1, HS, FH), F32),
        ),
        in_specs=[any_spec] * 4,
        out_specs=(pl.BlockSpec(memory_space=pltpu.VMEM), any_spec, any_spec),
        scratch_shapes=[
            vmem((F, HS), BF16),
            vmem((HS, F), BF16),
            vmem((CH, CR, W), BF16),
            vmem((CH, CR, FH), BF16),
            vmem((CH, 2 * CR, HS), BF16),
            vmem((CH, CR, HS), F32),
            vmem((CH, 4, CR, FQ), F32),
            vmem((CH, 3, 2, HALF, FQ), BF16),
            vmem((CH, 3, 2, HALF, FQ), BF16),
            vmem((CH, CR, F), BF16),
            vmem((CH, CR, FH), BF16),
            vmem((CH, 2 * CR, HS), BF16),
            vmem((FH, HS), F32),
            vmem((HS, FH), F32),
            vmem((CH, CR, FQ), BF16),
            vmem((MEMBERS, 64, FQ), BF16),
            vmem((64, 128), F32),
            vmem((3, 16, 128), F32),
            dma((5,)),
            dma((2,)),
            dma((3,)),
            dma((3,)),
            dma((8,)),
            dma((8,)),
            dma((4, 4)),
            dma((4, 4)),
            dma((CH, 3, 2)),
            dma((CH, 3, 2)),
            dma((CH, 4)),
            dma((CH, 4)),
            dma((4, CH)),
            dma((4, CH)),
            dma((CH, 8)),
            dma((MEMBERS, 2)),
            dma((2,)),
            dma((3,)),
            dma((3,)),
        ],
        compiler_params=pltpu.CompilerParams(
            collective_id=0, has_side_effects=True, vmem_limit_bytes=60 * 1024 * 1024
        ),
        name="ensemble",
    )(rows_in, target, w_in, w_out)
    return reward.reshape(16), grad_in, grad_out


def solution(mesh):
    return jax.shard_map(
        per_device,
        mesh=mesh,
        in_specs=(
            P(("batch", "member", "tensor"), None),
            P(("batch", "member"), "tensor"),
            P("member", None, "tensor"),
            P("member", "tensor", None),
        ),
        out_specs=(
            P(("batch", "member", "tensor")),
            P("member", "batch", "tensor"),
            P("member", "tensor", "batch"),
        ),
        check_vma=False,
    )
```

```python
import jax
import jax.numpy as jnp
from jax import lax
from jax.experimental import pallas as pl
from jax.experimental.pallas import tpu as pltpu
from jax.sharding import PartitionSpec as P

MESH = pl.DeviceIdType.MESH
F32 = jnp.float32
BF16 = jnp.bfloat16

F = 1536
FH = F // 2
FQ = F // 4
HS = 1024
CH = 4
CR = 256
HALF = CR // 2
GR = CR // 4
W = F + FQ
MEMBERS = 16
SCALE = 2048.0**-0.5


def dot(a, b):
    return lax.dot_general(a, b, (((1,), (0,)), ((), ())), preferred_element_type=F32)


def dot_nt(a, b):
    return lax.dot_general(a, b, (((1,), (1,)), ((), ())), preferred_element_type=F32)


def dot_tn(a, b):
    return lax.dot_general(a, b, (((0,), (0,)), ((), ())), preferred_element_type=F32)


def kernel(
    rows_hbm, target_hbm, w_in_hbm, w_out_hbm,
    reward_ref, acc_in, acc_out,
    w_in, w_out, rows, rows_o, hid, slope, part, sbuf, rbuf, err, err_o, pre,
    pred_b, gathered, spread, spread_r,
    loc_sem, zg_s, zg_r, p1_s, p1_r, p2_s, p2_r, rs_s, rs_r, ag_s, ag_r, core_s, core_r,
    rw_s, rw_r, rwl_sem, rz_s, rz_r,
):
    b = lax.axis_index("batch")
    m = lax.axis_index("member")
    t = lax.axis_index("tensor")
    y, x = m // 4, m % 4

    def z_dev(d):
        return (b, m, (t + d) % 4)

    def plane_dev(dy, dx):
        return (b, ((y + dy) % 4) * 4 + (x + dx) % 4, t)

    other = (1 - b, m, t)
    group_dev = [plane_dev(3, 0), plane_dev(1, 0), plane_dev(0, 3), plane_dev(0, 1)]

    def remote(src, dst, s, r, dev):
        return pltpu.make_async_remote_copy(
            src_ref=src, dst_ref=dst, send_sem=s, recv_sem=r, device_id=dev, device_id_type=MESH
        )

    def al(v, k):
        return pl.multiple_of(v, k)

    def quarter(q):
        return pl.ds(al((q % 4) * FQ, 128), FQ)

    mine_cols = pl.ds(al(b * FH, 128), FH)
    other_cols = pl.ds(al((1 - b) * FH, 128), FH)

    barrier = pltpu.get_barrier_semaphore()
    for d in range(1, 4):
        pl.semaphore_signal(barrier, inc=1, device_id=z_dev(d), device_id_type=MESH)
    pl.semaphore_signal(barrier, inc=1, device_id=other, device_id_type=MESH)

    @pl.loop(1, MEMBERS)
    def _(d):
        pl.semaphore_signal(
            barrier, inc=1, device_id=(b, (m + d) % MEMBERS, t), device_id_type=MESH
        )

    a_base = al(x * 32, 32)
    b_base = al(HALF + y * 32, 32)
    own_base = al(
        (1 - t // 2) * (x * 32 + t * 16) + (t // 2) * (HALF + y * 32 + (t - 2) * 16), 16
    )

    load_w_in = pltpu.make_async_copy(w_in_hbm.at[0], w_in, loc_sem.at[0])
    load_w_out = pltpu.make_async_copy(w_out_hbm.at[0], w_out, loc_sem.at[1])
    load_rows = pltpu.make_async_copy(
        rows_hbm, rows.at[0, pl.ds(own_base, 16), pl.ds(0, F)], loc_sem.at[2]
    )
    load_ta = pltpu.make_async_copy(
        target_hbm.at[pl.ds(0, 32)], rows.at[0, pl.ds(a_base, 32), pl.ds(F, FQ)], loc_sem.at[3]
    )
    load_tb = pltpu.make_async_copy(
        target_hbm.at[pl.ds(32, 32)], rows.at[0, pl.ds(b_base, 32), pl.ds(F, FQ)], loc_sem.at[4]
    )
    load_rows.start()
    load_ta.start()
    load_tb.start()
    load_w_in.start()
    load_w_out.start()

    pl.semaphore_wait(barrier, 3 + 1 + MEMBERS - 1)

    def z_gather(d):
        return remote(
            rows_hbm,
            rows.at[0, pl.ds(own_base, 16), pl.ds(0, F)],
            zg_s.at[d - 1],
            zg_r.at[d - 1],
            z_dev(d),
        )

    def z_gather_in(d):
        s = (t + 4 - d) % 4
        base = al((1 - s // 2) * (x * 32 + s * 16) + (s // 2) * (HALF + y * 32 + (s - 2) * 16), 16)
        return remote(
            rows_hbm,
            rows.at[0, pl.ds(base, 16), pl.ds(0, F)],
            zg_s.at[d - 1],
            zg_r.at[d - 1],
            z_dev(d),
        )

    for d in (2, 1, 3):
        z_gather(d).start()
    acc_in[...] = jnp.zeros_like(acc_in)
    acc_out[...] = jnp.zeros_like(acc_out)
    load_rows.wait()
    load_ta.wait()
    load_tb.wait()
    for d in (1, 3, 2):
        z_gather_in(d).wait_recv()

    def strip(axis, d):
        if axis == 0:
            return al(((x + d) % 4) * 32, 32)
        return al(HALF + ((y + d) % 4) * 32, 32)

    def axis_dev(axis, d):
        return plane_dev(0, d) if axis == 0 else plane_dev(d, 0)

    def phase1(axis, d):
        ref = rows.at[0, pl.ds(strip(axis, 0), 32)]
        k = axis * 4 + d // 2
        return remote(ref, ref, p1_s.at[k], p1_r.at[k], axis_dev(axis, d))

    def phase1_in(axis, d):
        ref = rows.at[0, pl.ds(strip(axis, 4 - d), 32)]
        k = axis * 4 + d // 2
        return remote(ref, ref, p1_s.at[k], p1_r.at[k], axis_dev(axis, d))

    def phase1_fwd(axis, d):
        ref = rows.at[0, pl.ds(al(strip(axis, 4 - d) + (d // 2) * 16, 16), 16)]
        k = axis * 4 + 2 + d // 2
        return remote(ref, ref, p1_s.at[k], p1_r.at[k], axis_dev(axis, d))

    def phase1_fwd_in(axis, d):
        ref = rows.at[0, pl.ds(al(strip(axis, 2) + (d // 2) * 16, 16), 16)]
        k = axis * 4 + 2 + d // 2
        return remote(ref, ref, p1_s.at[k], p1_r.at[k], axis_dev(axis, d))

    sides = [(0, 1), (0, 3), (1, 1), (1, 3)]
    for axis, d in sides:
        phase1(axis, d).start()
    for axis, d in sides:
        phase1_in(axis, d).wait_recv()
        phase1_fwd(axis, d).start()
    for axis, d in sides:
        phase1_fwd_in(axis, d).wait_recv()

    def phase2(c, g):
        src_chunk = 1 if c == 3 else 0
        src_group = g ^ 1 if c == 2 else g
        return remote(
            rows.at[src_chunk, pl.ds(src_group * GR, GR)],
            rows.at[c, pl.ds(g * GR, GR)],
            p2_s.at[c, g],
            p2_r.at[c, g],
            group_dev[g],
        )

    for c in (1, 2):
        for g in range(4):
            phase2(c, g).start()

    def core_copy(kind, c):
        src, dst = (
            (rows.at[c, :, other_cols], rows_o.at[c]),
            (hid.at[c, pl.ds(0, CR)], hid.at[c, pl.ds(CR, CR)]),
            (err.at[c, :, other_cols], err_o.at[c]),
            (pre.at[c, pl.ds(0, CR)], pre.at[c, pl.ds(CR, CR)]),
        )[kind]
        return remote(src, dst, core_s.at[kind, c], core_r.at[kind, c], other)

    def forward(c):
        core_copy(0, c).start()

        @pl.loop(0, HS // 256, unroll=True)
        def _(n):
            cols = pl.ds(al(n * 256, 256), 256)
            v = dot(rows[c, :, pl.ds(0, F)], w_in[:, cols])
            s = jax.nn.sigmoid(v)
            hid[c, pl.ds(0, CR), cols] = (v * s).astype(BF16)
            slope[c, :, cols] = s * (1.0 + v * (1.0 - s))

        core_copy(1, c).start()
        for rel in (3, 1, 2, 0):
            part[c, rel] = dot(hid[c, pl.ds(0, CR)], w_out[:, quarter(t + rel)])
            if rel == 3:
                sbuf[c, 0, 0] = part[c, 3, pl.ds(0, HALF)].astype(BF16)
            elif rel == 1:
                sbuf[c, 0, 1] = part[c, 1, pl.ds(HALF, HALF)].astype(BF16)

    def rs_start(c):
        rs(c, 0, 0).start()
        rs(c, 0, 1).start()

    def rs(c, s, way):
        return remote(
            sbuf.at[c, s, way], rbuf.at[c, s, way], rs_s.at[c, s, way], rs_r.at[c, s, way],
            z_dev(1 if way == 0 else 3),
        )

    def rs_step(c, s):
        for way in range(2):
            rs(c, s - 1, way).wait_recv()
            rel = (3 - s) if way == 0 else (1 + s)
            own = part[c, rel, pl.ds(way * HALF, HALF)]
            sbuf[c, s, way] = (own + rbuf[c, s - 1, way].astype(F32)).astype(BF16)
            rs(c, s, way).start()

    def ag(c, way):
        ref = err.at[c, :, quarter(t)]
        return remote(ref, ref, ag_s.at[c, way], ag_r.at[c, way], z_dev(1 if way == 0 else 3))

    def ag_in(c, way):
        ref = err.at[c, :, quarter(t + (3 if way == 0 else 1))]
        return remote(ref, ref, ag_s.at[c, way], ag_r.at[c, way], z_dev(1 if way == 0 else 3))

    def ag_fwd(c, way):
        ref = err.at[c, pl.ds(way * HALF, HALF), quarter(t + (3 if way == 0 else 1))]
        k = 2 + way
        return remote(ref, ref, ag_s.at[c, k], ag_r.at[c, k], z_dev(1 if way == 0 else 3))

    def ag_fwd_in(c, way):
        ref = err.at[c, pl.ds(way * HALF, HALF), quarter(t + 2)]
        k = 2 + way
        return remote(ref, ref, ag_s.at[c, k], ag_r.at[c, k], z_dev(1 if way == 0 else 3))

    def reward_piece(c, p):
        first, second = (c + 1) // 2, (4 - (c + 1) // 2) % 4
        away = first if p % 4 < 2 else second
        idx = (p % 4 + 2 * ((c // 2) * (1 - c // 3))) % 4
        if p < 4:
            owner = ((y + away) % 4) * 4 + idx
        else:
            owner = idx * 4 + (x + away) % 4
        src = pred_b.at[c, pl.ds(32 * p, 32)]
        dst = gathered.at[m, pl.ds(32 * (p // 4), 32)]
        return owner, src, dst

    def reward_send(c):
        for p in range(8):
            owner, src, dst = reward_piece(c, p)

            @pl.when(owner != m)
            def _():
                remote(
                    src, dst, rw_s.at[c, p], rw_r.at[m, p // 4], (b, owner, t)
                ).start()

            @pl.when(owner == m)
            def _():
                pltpu.make_async_copy(src, dst, rwl_sem.at[p // 4]).start()

    def errors(c):
        for way in range(2):
            rs(c, 2, way).wait_recv()
            r = pl.ds(way * HALF, HALF)
            pred = part[c, 0, r] + rbuf[c, 2, way].astype(F32)
            goal = rows[c, r, pl.ds(F, FQ)].astype(F32)
            err[c, r, quarter(t)] = ((pred - goal) * SCALE).astype(BF16)
            pred_b[c, r] = pred.astype(BF16)
        ag(c, 0).start()
        ag(c, 1).start()

    def ag_forward(c):
        for way in range(2):
            ag_in(c, way).wait_recv()
            ag_fwd(c, way).start()

    def back(c):
        for way in range(2):
            ag_fwd_in(c, way).wait_recv()
        core_copy(2, c).start()

        @pl.loop(0, HS // 256, unroll=True)
        def _(n):
            cols = pl.ds(al(n * 256, 256), 256)
            g = dot_nt(err[c], w_out[cols, :])
            pre[c, pl.ds(0, CR), cols] = (g * slope[c, :, cols]).astype(BF16)

        core_copy(3, c).start()

    def grads(c):
        core_copy(1, c).wait_recv()
        core_copy(2, c).wait_recv()

        @pl.loop(0, HS // 256, unroll=True)
        def _(n):
            cols = pl.ds(al(n * 256, 256), 256)
            acc_out[0, cols, :] += dot_tn(hid[c, pl.ds(0, CR), cols], err[c, :, mine_cols]) + dot_tn(
                hid[c, pl.ds(CR, CR), cols], err_o[c]
            )

        core_copy(0, c).wait_recv()
        core_copy(3, c).wait_recv()

        @pl.loop(0, FH // 256, unroll=True)
        def _(n):
            here = pl.ds(al(b * FH + n * 256, 128), 256)
            cols = pl.ds(al(n * 256, 256), 256)
            acc_in[0, cols, :] += dot_tn(rows[c, :, here], pre[c, pl.ds(0, CR)]) + dot_tn(
                rows_o[c, :, cols], pre[c, pl.ds(CR, CR)]
            )

    load_w_in.wait()
    load_w_out.wait()
    forward(0)
    rs_start(0)

    def tick(i, carry):
        @pl.when(i >= 1)
        def _():
            errors(i - 1)

        @pl.when(i >= 2)
        def _():
            back(i - 2)

        rs_step(i, 1)

        @pl.when(i < CH - 1)
        def _():
            for g in range(4):
                remote(
                    rows.at[0, pl.ds(0, GR)],
                    rows.at[i + 1, pl.ds(g * GR, GR)],
                    p2_s.at[i + 1, g],
                    p2_r.at[i + 1, g],
                    group_dev[g],
                ).wait_recv()

            @pl.when(i == 0)
            def _():
                for g in range(4):
                    phase2(3, g).start()

            forward(i + 1)

            @pl.when(i == 0)
            def _():
                rs_start(1)

        @pl.when(i >= 1)
        def _():
            ag_forward(i - 1)

        rs_step(i, 2)

        @pl.when((i >= 1) & (i < CH - 1))
        def _():
            rs_start(i + 1)

        @pl.when(i >= 1)
        def _():
            reward_send(i - 1)

        @pl.when(i >= 2)
        def _():
            grads(i - 2)

        return carry

    lax.fori_loop(0, CH, tick, 0)
    errors(CH - 1)
    back(CH - 2)
    reward_send(CH - 1)
    grads(CH - 2)
    ag_forward(CH - 1)

    for d in range(1, 4):
        z_gather(d).wait_send()
    for axis, d in sides:
        phase1(axis, d).wait_send()
        phase1_fwd(axis, d).wait_send()
    for c in (1, 2, 3):
        for g in range(4):
            phase2(c, g).wait_send()

    def sent(c, last):
        for way in range(2):
            for s in range(3):
                rs(c, s, way).wait_send()
            ag(c, way).wait_send()
            if not last:
                ag_fwd(c, way).wait_send()
        for kind in range(4):
            if not (last and kind >= 2):
                core_copy(kind, c).wait_send()
        for p in range(8):
            owner, src, dst = reward_piece(c, p)

            @pl.when(owner != m)
            def _():
                remote(src, dst, rw_s.at[c, p], rw_r.at[m, p // 4], (b, owner, t)).wait_send()

    @pl.loop(0, CH - 1)
    def _(c):
        sent(c, False)

    sent(CH - 1, True)

    def reward_in(s, half):
        return remote(
            pred_b.at[0, pl.ds(0, 32)],
            gathered.at[s, pl.ds(32 * half, 32)],
            rw_s.at[0, 0],
            rw_r.at[s, half],
            (b, s, t),
        )

    @pl.loop(0, MEMBERS)
    def _(s):
        @pl.when(s != m)
        def _():
            for half in range(2):
                reward_in(s, half).wait_recv()

        @pl.when(s == m)
        def _():
            for half in range(2):
                pltpu.make_async_copy(
                    pred_b.at[0, pl.ds(0, 32)],
                    gathered.at[s, pl.ds(32 * half, 32)],
                    rwl_sem.at[half],
                ).wait()

    total = jnp.zeros((64, 128), F32)
    for k in range(3):
        cols = pl.ds(128 * k, 128)
        mean = jnp.zeros((64, 128), F32)
        for s in range(MEMBERS):
            mean += gathered[s, :, cols].astype(F32)
        mean = mean * (1.0 / MEMBERS)
        for s in range(MEMBERS):
            dev = gathered[s, :, cols].astype(F32) - mean
            total += dev * dev
    spread[...] = total

    def spread_copy(d):
        return remote(
            spread.at[pl.ds(al(((t + d) % 4) * 16, 16), 16)],
            spread_r.at[d - 1],
            rz_s.at[d - 1],
            rz_r.at[d - 1],
            z_dev(d),
        )

    for d in range(1, 4):
        spread_copy(d).start()

    back(CH - 1)
    grads(CH - 1)

    for d in range(1, 4):
        spread_copy(d).wait_recv()
    own = spread[pl.ds(al(t * 16, 16), 16)]
    for d in range(3):
        own += spread_r[d]
    reward_ref[...] = jnp.sum(own.T, axis=0, keepdims=True) * (1.0 / (MEMBERS * F))

    for d in range(1, 4):
        spread_copy(d).wait_send()
    for way in range(2):
        ag_fwd(CH - 1, way).wait_send()
    for kind in (2, 3):
        core_copy(kind, CH - 1).wait_send()


def per_device(rows_in, target, w_in, w_out):
    any_spec = pl.BlockSpec(memory_space=pl.ANY)
    vmem = pltpu.VMEM
    dma = pltpu.SemaphoreType.DMA
    reward, grad_in, grad_out = pl.pallas_call(
        kernel,
        out_shape=(
            vmem((1, 16), F32),
            vmem((1, FH, HS), F32),
            vmem((1, HS, FH), F32),
        ),
        in_specs=[any_spec] * 4,
        out_specs=(pl.BlockSpec(memory_space=pltpu.VMEM),) * 3,
        scratch_shapes=[
            vmem((F, HS), BF16),
            vmem((HS, F), BF16),
            vmem((CH, CR, W), BF16),
            vmem((CH, CR, FH), BF16),
            vmem((CH, 2 * CR, HS), BF16),
            vmem((CH, CR, HS), F32),
            vmem((CH, 4, CR, FQ), F32),
            vmem((CH, 3, 2, HALF, FQ), BF16),
            vmem((CH, 3, 2, HALF, FQ), BF16),
            vmem((CH, CR, F), BF16),
            vmem((CH, CR, FH), BF16),
            vmem((CH, 2 * CR, HS), BF16),
            vmem((CH, CR, FQ), BF16),
            vmem((MEMBERS, 64, FQ), BF16),
            vmem((64, 128), F32),
            vmem((3, 16, 128), F32),
            dma((5,)),
            dma((3,)),
            dma((3,)),
            dma((8,)),
            dma((8,)),
            dma((4, 4)),
            dma((4, 4)),
            dma((CH, 3, 2)),
            dma((CH, 3, 2)),
            dma((CH, 4)),
            dma((CH, 4)),
            dma((4, CH)),
            dma((4, CH)),
            dma((CH, 8)),
            dma((MEMBERS, 2)),
            dma((2,)),
            dma((3,)),
            dma((3,)),
        ],
        compiler_params=pltpu.CompilerParams(
            collective_id=0, has_side_effects=True, vmem_limit_bytes=54 * 1024 * 1024
        ),
        name="ensemble",
    )(rows_in, target, w_in, w_out)
    return reward.reshape(16), grad_in, grad_out


def solution(mesh):
    return jax.shard_map(
        per_device,
        mesh=mesh,
        in_specs=(
            P(("batch", "member", "tensor"), None),
            P(("batch", "member"), "tensor"),
            P("member", None, "tensor"),
            P("member", "tensor", None),
        ),
        out_specs=(
            P(("batch", "member", "tensor")),
            P("member", "batch", "tensor"),
            P("member", "tensor", "batch"),
        ),
        check_vma=False,
    )
```

```python
import jax
import jax.numpy as jnp
from jax import lax
from jax.experimental import pallas as pl
from jax.experimental.pallas import tpu as pltpu
from jax.sharding import PartitionSpec as P

MESH = pl.DeviceIdType.MESH
F32 = jnp.float32
BF16 = jnp.bfloat16

F = 1536
FH = F // 2
FQ = F // 4
HS = 1024
R = 1024
W = F + FQ
ST = 32
MEMBERS = 16
SCALE = 2048.0**-0.5

CHUNKS = (
    ("A00", "B00"),
    ("A01", "A03", "B10", "B30"),
    ("A10", "A30", "B01", "B03"),
    ("A11", "A13", "A31", "A33", "B11", "B31", "B13", "B33"),
    ("A02", "A12", "A32", "B20", "B21", "B23"),
    ("A20", "A23", "B02", "B32"),
    ("A21", "A22", "B12", "B22"),
)
STRIPS = tuple(s for chunk in CHUNKS for s in chunk)
POS = {s: ST * k for k, s in enumerate(STRIPS)}
SIZE = tuple(ST * len(chunk) for chunk in CHUNKS)
OFF = tuple(sum(SIZE[:c]) for c in range(len(CHUNKS)))
NC = len(CHUNKS)
GROUPS = ((0, 1, 2), (3,), (4,), (5, 6))
NG = len(GROUPS)

HOPS = (
    ("p1", "A00", 0, 32, "A03", (0, 1)),
    ("p1", "A00", 0, 32, "A01", (0, 3)),
    ("p1", "B00", 0, 32, "B30", (1, 0)),
    ("p1", "B00", 0, 32, "B10", (3, 0)),
    ("p2", "A00", 0, 32, "A30", (1, 0)),
    ("p2", "A00", 0, 32, "A10", (3, 0)),
    ("p2", "B00", 0, 32, "B03", (0, 1)),
    ("p2", "B00", 0, 32, "B01", (0, 3)),
    ("d", "A03", 0, 16, "A02", (0, 1)),
    ("d", "A01", 16, 16, "A02", (0, 3)),
    ("d", "B30", 0, 16, "B20", (1, 0)),
    ("d", "B10", 16, 16, "B20", (3, 0)),
    ("q3", "A01", 0, 64, "A31", (1, 0)),
    ("q3", "A01", 0, 64, "A11", (3, 0)),
    ("q3", "B10", 0, 64, "B13", (0, 1)),
    ("q3", "B10", 0, 64, "B11", (0, 3)),
    ("q4", "A02", 0, 32, "A32", (1, 0)),
    ("q4", "A02", 0, 32, "A12", (3, 0)),
    ("q4", "B20", 0, 32, "B23", (0, 1)),
    ("q4", "B20", 0, 32, "B21", (0, 3)),
    ("q5", "A33", 0, 32, "A23", (1, 0)),
    ("q5", "A10", 0, 32, "A20", (3, 0)),
    ("q5", "B33", 0, 32, "B32", (0, 1)),
    ("q5", "B01", 0, 32, "B02", (0, 3)),
    ("q6", "A32", 0, 32, "A22", (1, 0)),
    ("q6", "A11", 0, 32, "A21", (3, 0)),
    ("q6", "B23", 0, 32, "B22", (0, 1)),
    ("q6", "B11", 0, 32, "B12", (0, 3)),
)
NEEDS = ((), ("p1",), ("p2",), ("q3",), ("d", "q4"), ("q5",), ("q6",))
RELAY = {
    "X1": (("p1",), ("d", "q3")),
    "X2": (("d",), ("q4",)),
    "X3": (("p2", "q3"), ("q5",)),
    "X4": (("q3", "q4"), ("q6",)),
}
ORDER = (
    "P1", "F0", "G0", "H0", "R0", "X1", "F1", "G1", "S0", "F2", "G2", "H2", "H1", "R1", "X2",
    "E0", "R2", "S1", "A0", "F3", "S2", "X3", "G3", "E1", "F4", "E2", "G4", "H3", "F5", "X4",
    "H5", "H4", "G5", "W1", "R3", "A2", "R4", "F6", "A1", "H6", "S3", "G6", "W2", "S4", "R5",
    "B0", "E3", "W0", "R6", "A3", "S5", "I0", "S6", "E4", "O0", "E5", "W5", "E6", "B1", "A4",
    "W4", "W3", "A5", "O1", "A6", "W6", "I1", "B2", "T1", "B3", "Y1", "O2", "I2", "I3", "O3",
    "Y2",
)


def dot(a, b):
    return lax.dot_general(a, b, (((1,), (0,)), ((), ())), preferred_element_type=F32)


def dot_nt(a, b):
    return lax.dot_general(a, b, (((1,), (1,)), ((), ())), preferred_element_type=F32)


def dot_tn(a, b):
    return lax.dot_general(a, b, (((0,), (0,)), ((), ())), preferred_element_type=F32)


def kernel(
    rows_hbm, target_hbm, w_in_hbm, w_out_hbm,
    reward_ref, acc_in, acc_out,
    w_in, w_out, rows, rows_o, hid, slope, part, sbuf, rbuf, err, err_o, pre,
    pred_b, gathered, spread, spread_r,
    loc_sem, zg_s, zg_r, xy_s, xy_r, rs_s, rs_r, ag_s, ag_r, core_s, core_r, grp_s, grp_r,
    rw_s, rw_r, rwl_sem, rz_s, rz_r,
):
    b = lax.axis_index("batch")
    m = lax.axis_index("member")
    t = lax.axis_index("tensor")
    y, x = m // 4, m % 4

    def z_dev(d):
        return (b, m, (t + d) % 4)

    def plane_dev(dy, dx):
        return (b, ((y + dy) % 4) * 4 + (x + dx) % 4, t)

    other = (1 - b, m, t)

    def remote(src, dst, s, r, dev):
        return pltpu.make_async_remote_copy(
            src_ref=src, dst_ref=dst, send_sem=s, recv_sem=r, device_id=dev, device_id_type=MESH
        )

    started = []

    def go(copy):
        copy.start()
        started.append(copy)

    def al(v, k):
        return pl.multiple_of(v, k)

    def quarter(q):
        return pl.ds(al((q % 4) * FQ, 128), FQ)

    mine_cols = pl.ds(al(b * FH, 128), FH)
    other_cols = pl.ds(al((1 - b) * FH, 128), FH)

    barrier = pltpu.get_barrier_semaphore()
    for d in range(1, 4):
        pl.semaphore_signal(barrier, inc=1, device_id=z_dev(d), device_id_type=MESH)
    pl.semaphore_signal(barrier, inc=1, device_id=other, device_id_type=MESH)

    @pl.loop(1, MEMBERS)
    def _(d):
        pl.semaphore_signal(
            barrier, inc=1, device_id=(b, (m + d) % MEMBERS, t), device_id_type=MESH
        )

    own_rows = rows.at[pl.ds(al(t * 16, 16), 16), pl.ds(0, F)]
    load_rows = pltpu.make_async_copy(rows_hbm, own_rows, loc_sem.at[0])
    load_target = pltpu.make_async_copy(
        target_hbm, rows.at[pl.ds(0, 64), pl.ds(F, FQ)], loc_sem.at[1]
    )
    load_w_in = pltpu.make_async_copy(w_in_hbm.at[0], w_in, loc_sem.at[2])
    load_w_out = pltpu.make_async_copy(w_out_hbm.at[0], w_out, loc_sem.at[3])
    load_rows.start()
    load_target.start()
    load_w_in.start()
    load_w_out.start()
    pl.semaphore_wait(barrier, 3 + 1 + MEMBERS - 1)

    for d in (2, 1, 3):
        go(remote(rows_hbm, own_rows, zg_s.at[d - 1], zg_r.at[d - 1], z_dev(d)))
    load_rows.wait()
    load_target.wait()
    for d in (1, 3, 2):
        theirs = rows.at[pl.ds(al(((t + 4 - d) % 4) * 16, 16), 16), pl.ds(0, F)]
        remote(rows_hbm, theirs, zg_s.at[d - 1], zg_r.at[d - 1], z_dev(d)).wait_recv()

    def hop(k):
        _, first, skip, n, land, (dy, dx) = HOPS[k]
        return remote(
            rows.at[pl.ds(POS[first] + skip, n)],
            rows.at[pl.ds(POS[land] + skip, n)],
            xy_s.at[k],
            xy_r.at[k],
            plane_dev(dy, dx),
        )

    here = set()

    def arrived(names):
        for name in names:
            if name not in here:
                here.add(name)
                for k in range(len(HOPS)):
                    if HOPS[k][0] == name:
                        hop(k).wait_recv()

    def send_hops(names):
        for name in names:
            for k in range(len(HOPS)):
                if HOPS[k][0] == name:
                    go(hop(k))

    def core_copy(kind, c):
        r = pl.ds(OFF[c], SIZE[c])
        if kind == 0:
            src, dst = rows.at[r, other_cols], rows_o.at[r]
        else:
            src, dst = hid.at[0, r], hid.at[1, r]
        return remote(src, dst, core_s.at[kind, c], core_r.at[kind, c], other)

    def forward(c):
        arrived(NEEDS[c])
        if c == 0:
            load_w_in.wait()
        r = pl.ds(OFF[c], SIZE[c])
        go(core_copy(0, c))

        @pl.loop(0, HS // 256, unroll=True)
        def _(n):
            cols = pl.ds(al(n * 256, 256), 256)
            v = dot(rows[r, pl.ds(0, F)], w_in[:, cols])
            s = jax.nn.sigmoid(v)
            hid[0, r, cols] = (v * s).astype(BF16)
            slope[r, cols] = s * (1.0 + v * (1.0 - s))

        go(core_copy(1, c))

    def halves(c, way):
        h = SIZE[c] // 2
        return pl.ds(OFF[c] + way * h, h), pl.ds(OFF[c] // 2, h)

    def predict(c, rel):
        r = pl.ds(OFF[c], SIZE[c])
        part[rel, r] = dot(hid[0, r], w_out[:, quarter(t + rel)])

    def predict_first(c):
        if c == 0:
            load_w_out.wait()
        for way, rel in ((0, 3), (1, 1)):
            predict(c, rel)
            r, q = halves(c, way)
            sbuf[0, way, q] = part[rel, r].astype(BF16)
            go(rs(c, 0, way))

    def rs(c, s, way):
        _, q = halves(c, way)
        return remote(
            sbuf.at[s, way, q], rbuf.at[s, way, q], rs_s.at[c, s, way], rs_r.at[c, s, way],
            z_dev(1 + 2 * way),
        )

    def rs_step(c, s):
        for way in range(2):
            rs(c, s - 1, way).wait_recv()
            rel = (3 - s) if way == 0 else (1 + s)
            r, q = halves(c, way)
            sbuf[s, way, q] = (part[rel, r] + rbuf[s - 1, way, q].astype(F32)).astype(BF16)
            go(rs(c, s, way))

    def ag_copy(c, k, way, incoming):
        r, _ = halves(c, way if k != 1 else 1 - way)
        source = t if k < 2 else t + 3 - 2 * way
        if incoming:
            source = source + 3 - 2 * way
        ref = err.at[r, quarter(source)]
        return remote(ref, ref, ag_s.at[c, k, way], ag_r.at[c, k, way], z_dev(1 + 2 * way))

    def errors(c):
        for way in range(2):
            rs(c, 2, way).wait_recv()
            r, q = halves(c, way)
            pred = part[0, r] + rbuf[2, way, q].astype(F32)
            goal = rows[r, pl.ds(F, FQ)].astype(F32)
            err[r, quarter(t)] = ((pred - goal) * SCALE).astype(BF16)
            pred_b[r] = pred.astype(BF16)
            go(ag_copy(c, 0, way, False))
        for way in range(2):
            go(ag_copy(c, 1, way, False))

    def ag_forward(c):
        for way in range(2):
            ag_copy(c, 0, way, True).wait_recv()
            go(ag_copy(c, 2, way, False))

    def reward_send(c):
        for strip in CHUNKS[c]:
            half, dy, dx = int(strip[0] == "B"), int(strip[1]), int(strip[2])
            k = POS[strip] // ST
            src = pred_b.at[pl.ds(POS[strip], ST)]
            dst = gathered.at[m, pl.ds(ST * half, ST)]
            if (dy, dx) == (0, 0):
                pltpu.make_async_copy(src, dst, rwl_sem.at[half]).start()
            else:
                go(remote(src, dst, rw_s.at[k], rw_r.at[m, half], plane_dev(dy, dx)))

    def group_rows(g):
        c0, c1 = GROUPS[g][0], GROUPS[g][-1]
        return pl.ds(OFF[c0], OFF[c1] + SIZE[c1] - OFF[c0])

    def group_copy(kind, g):
        r = group_rows(g)
        if kind == 0:
            src, dst = err.at[r, other_cols], err_o.at[r]
        else:
            src, dst = pre.at[0, r], pre.at[1, r]
        return remote(src, dst, grp_s.at[kind, g], grp_r.at[kind, g], other)

    def back(g):
        for c in GROUPS[g]:
            for k in (1, 2):
                for way in range(2):
                    ag_copy(c, k, way, True).wait_recv()
        go(group_copy(0, g))
        r = group_rows(g)

        @pl.loop(0, HS // 256, unroll=True)
        def _(n):
            cols = pl.ds(al(n * 256, 256), 256)
            v = dot_nt(err[r], w_out[cols, :])
            pre[0, r, cols] = (v * slope[r, cols]).astype(BF16)

        go(group_copy(1, g))

    begun = set()

    def grad_out(g):
        for c in GROUPS[g]:
            core_copy(1, c).wait_recv()
        group_copy(0, g).wait_recv()
        r = group_rows(g)
        first = "out" not in begun
        begun.add("out")

        @pl.loop(0, HS // 256, unroll=True)
        def _(n):
            cols = pl.ds(al(n * 256, 256), 256)
            v = dot_tn(hid[0, r, cols], err[r, mine_cols]) + dot_tn(hid[1, r, cols], err_o[r])
            acc_out[0, cols, :] = v if first else acc_out[0, cols, :] + v

    def grad_in(g):
        for c in GROUPS[g]:
            core_copy(0, c).wait_recv()
        group_copy(1, g).wait_recv()
        r = group_rows(g)
        first = "in" not in begun
        begun.add("in")

        @pl.loop(0, FH // 256, unroll=True)
        def _(n):
            mine = pl.ds(al(b * FH + n * 256, 128), 256)
            cols = pl.ds(al(n * 256, 256), 256)
            v = dot_tn(rows[r, mine], pre[0, r]) + dot_tn(rows_o[r, cols], pre[1, r])
            acc_in[0, cols, :] = v if first else acc_in[0, cols, :] + v

    def spread_copy(d):
        return remote(
            spread.at[pl.ds(al(((t + d) % 4) * 16, 16), 16)],
            spread_r.at[d - 1],
            rz_s.at[d - 1],
            rz_r.at[d - 1],
            z_dev(d),
        )

    def reward_first():
        @pl.loop(1, MEMBERS)
        def _(d):
            s = (m + d) % MEMBERS
            for half in range(2):
                remote(
                    pred_b.at[pl.ds(0, ST)],
                    gathered.at[s, pl.ds(ST * half, ST)],
                    rw_s.at[2],
                    rw_r.at[s, half],
                    (b, s, t),
                ).wait_recv()

        for half in range(2):
            pltpu.make_async_copy(
                pred_b.at[pl.ds(ST * half, ST)],
                gathered.at[m, pl.ds(ST * half, ST)],
                rwl_sem.at[half],
            ).wait()

        total = jnp.zeros((64, 128), F32)
        for k in range(3):
            cols = pl.ds(128 * k, 128)
            mean = jnp.zeros((64, 128), F32)
            for s in range(MEMBERS):
                mean += gathered[s, :, cols].astype(F32)
            mean = mean * (1.0 / MEMBERS)
            for s in range(MEMBERS):
                dev = gathered[s, :, cols].astype(F32) - mean
                total += dev * dev
        spread[...] = total
        for d in range(1, 4):
            go(spread_copy(d))

    def reward_last():
        for d in range(1, 4):
            spread_copy(d).wait_recv()
        own = spread[pl.ds(al(t * 16, 16), 16)]
        for d in range(3):
            own += spread_r[d]
        reward_ref[...] = jnp.sum(own.T, axis=0, keepdims=True) * (1.0 / (MEMBERS * F))

    def sent(keep):
        while len(started) > keep:
            started.pop(0).wait_send()

    for step in ORDER:
        kind, k = step[0], int(step[1:])
        if kind == "P":
            send_hops(("p1", "p2"))
        elif kind == "X":
            arrived(RELAY[step][0])
            send_hops(RELAY[step][1])
        elif kind == "F":
            forward(k)
        elif kind == "G":
            predict_first(k)
        elif kind == "H":
            predict(k, 2)
            predict(k, 0)
        elif kind == "R":
            rs_step(k, 1)
        elif kind == "S":
            rs_step(k, 2)
        elif kind == "E":
            errors(k)
        elif kind == "A":
            ag_forward(k)
        elif kind == "W":
            reward_send(k)
        elif kind == "B":
            back(k)
        elif kind == "O":
            grad_out(k)
        elif kind == "I":
            grad_in(k)
        elif kind == "T":
            sent(16)
        elif step == "Y1":
            reward_first()
        else:
            reward_last()
    sent(0)


def per_device(rows_in, target, w_in, w_out):
    any_spec = pl.BlockSpec(memory_space=pl.ANY)
    vmem = pltpu.VMEM
    dma = pltpu.SemaphoreType.DMA
    reward, grad_in, grad_out = pl.pallas_call(
        kernel,
        out_shape=(
            vmem((1, 16), F32),
            vmem((1, FH, HS), F32),
            vmem((1, HS, FH), F32),
        ),
        in_specs=[any_spec] * 4,
        out_specs=(pl.BlockSpec(memory_space=pltpu.VMEM),) * 3,
        scratch_shapes=[
            vmem((F, HS), BF16),
            vmem((HS, F), BF16),
            vmem((R, W), BF16),
            vmem((R, FH), BF16),
            vmem((2, R, HS), BF16),
            vmem((R, HS), F32),
            vmem((4, R, FQ), F32),
            vmem((3, 2, R // 2, FQ), BF16),
            vmem((3, 2, R // 2, FQ), BF16),
            vmem((R, F), BF16),
            vmem((R, FH), BF16),
            vmem((2, R, HS), BF16),
            vmem((R, FQ), BF16),
            vmem((MEMBERS, 64, FQ), BF16),
            vmem((64, 128), F32),
            vmem((3, 16, 128), F32),
            dma((4,)),
            dma((3,)),
            dma((3,)),
            dma((len(HOPS),)),
            dma((len(HOPS),)),
            dma((NC, 3, 2)),
            dma((NC, 3, 2)),
            dma((NC, 3, 2)),
            dma((NC, 3, 2)),
            dma((2, NC)),
            dma((2, NC)),
            dma((2, NG)),
            dma((2, NG)),
            dma((len(STRIPS),)),
            dma((MEMBERS, 2)),
            dma((2,)),
            dma((3,)),
            dma((3,)),
        ],
        compiler_params=pltpu.CompilerParams(
            collective_id=0, has_side_effects=True, vmem_limit_bytes=54 * 1024 * 1024
        ),
        name="ensemble",
    )(rows_in, target, w_in, w_out)
    return reward.reshape(16), grad_in, grad_out


def solution(mesh):
    return jax.shard_map(
        per_device,
        mesh=mesh,
        in_specs=(
            P(("batch", "member", "tensor"), None),
            P(("batch", "member"), "tensor"),
            P("member", None, "tensor"),
            P("member", "tensor", None),
        ),
        out_specs=(
            P(("batch", "member", "tensor")),
            P("member", "batch", "tensor"),
            P("member", "tensor", "batch"),
        ),
        check_vma=False,
    )
```

```python
import jax
import jax.numpy as jnp
from jax import lax
from jax.experimental import pallas as pl
from jax.experimental.pallas import tpu as pltpu
from jax.sharding import PartitionSpec as P

MESH = pl.DeviceIdType.MESH
F32 = jnp.float32
BF16 = jnp.bfloat16

F = 1536
FH = F // 2
FQ = F // 4
HS = 1024
R = 1024
W = F + FQ
ST = 32
MEMBERS = 16
SCALE = 2048.0**-0.5

CHUNKS = (
    ("A00", "B00"),
    ("A01", "A03", "B10", "B30"),
    ("A10", "A30", "B01", "B03"),
    ("A11", "A13", "A31", "A33", "B11", "B31", "B13", "B33"),
    ("A02", "A12", "A32", "B20", "B21", "B23"),
    ("A20", "A23", "B02", "B32"),
    ("A21", "A22", "B12", "B22"),
)
STRIPS = tuple(s for chunk in CHUNKS for s in chunk)
POS = {s: ST * k for k, s in enumerate(STRIPS)}
SIZE = tuple(ST * len(chunk) for chunk in CHUNKS)
OFF = tuple(sum(SIZE[:c]) for c in range(len(CHUNKS)))
NC = len(CHUNKS)
GROUPS = ((0, 1, 2), (3,), (4,), (5, 6))
NG = len(GROUPS)

HOPS = (
    ("p1", "A00", 0, 32, "A03", (0, 1)),
    ("p1", "A00", 0, 32, "A01", (0, 3)),
    ("p1", "B00", 0, 32, "B30", (1, 0)),
    ("p1", "B00", 0, 32, "B10", (3, 0)),
    ("p2", "A00", 0, 32, "A30", (1, 0)),
    ("p2", "A00", 0, 32, "A10", (3, 0)),
    ("p2", "B00", 0, 32, "B03", (0, 1)),
    ("p2", "B00", 0, 32, "B01", (0, 3)),
    ("d", "A03", 0, 16, "A02", (0, 1)),
    ("d", "A01", 16, 16, "A02", (0, 3)),
    ("d", "B30", 0, 16, "B20", (1, 0)),
    ("d", "B10", 16, 16, "B20", (3, 0)),
    ("q3", "A01", 0, 64, "A31", (1, 0)),
    ("q3", "A01", 0, 64, "A11", (3, 0)),
    ("q3", "B10", 0, 64, "B13", (0, 1)),
    ("q3", "B10", 0, 64, "B11", (0, 3)),
    ("q4", "A02", 0, 32, "A32", (1, 0)),
    ("q4", "A02", 0, 32, "A12", (3, 0)),
    ("q4", "B20", 0, 32, "B23", (0, 1)),
    ("q4", "B20", 0, 32, "B21", (0, 3)),
    ("q5", "A33", 0, 32, "A23", (1, 0)),
    ("q5", "A10", 0, 32, "A20", (3, 0)),
    ("q5", "B33", 0, 32, "B32", (0, 1)),
    ("q5", "B01", 0, 32, "B02", (0, 3)),
    ("q6", "A32", 0, 32, "A22", (1, 0)),
    ("q6", "A11", 0, 32, "A21", (3, 0)),
    ("q6", "B23", 0, 32, "B22", (0, 1)),
    ("q6", "B11", 0, 32, "B12", (0, 3)),
)
NEEDS = ((), ("p1",), ("p2",), ("q3",), ("d", "q4"), ("q5",), ("q6",))
RELAY = {
    "X1": (("p1",), ("d", "q3")),
    "X2": (("d",), ("q4",)),
    "X3": (("p2", "q3"), ("q5",)),
    "X4": (("q3", "q4"), ("q6",)),
}
ORDER = (
    "P1", "F0", "G0", "H0", "R0", "X1", "F1", "G1", "S0", "F2", "G2", "H2", "H1", "R1", "X2",
    "E0", "R2", "S1", "A0", "F3", "S2", "X3", "G3", "E1", "F4", "E2", "G4", "H3", "F5", "X4",
    "H5", "H4", "G5", "W1", "R3", "A2", "R4", "F6", "A1", "H6", "S3", "G6", "W2", "S4", "R5",
    "B0", "E3", "W0", "R6", "A3", "S5", "I0", "S6", "E4", "O0", "E5", "W5", "E6", "B1", "A4",
    "W4", "W3", "A5", "O1", "A6", "W6", "I1", "B2", "T1", "B3", "Y1", "O2", "I2", "I3", "O3",
    "Y2",
)


def dot(a, b):
    return lax.dot_general(a, b, (((1,), (0,)), ((), ())), preferred_element_type=F32)


def dot_nt(a, b):
    return lax.dot_general(a, b, (((1,), (1,)), ((), ())), preferred_element_type=F32)


def dot_tn(a, b):
    return lax.dot_general(a, b, (((0,), (0,)), ((), ())), preferred_element_type=F32)


def kernel(
    rows_hbm, target_hbm, w_in_hbm, w_out_hbm,
    reward_ref, acc_in, acc_out,
    w_in, w_out, rows, rows_o, hid, slope, part, sbuf, rbuf, err, err_o, pre,
    pred_b, gathered, spread, spread_r,
    loc_sem, zg_s, zg_r, xy_s, xy_r, rs_s, rs_r, ag_s, ag_r, core_s, core_r, grp_s, grp_r,
    rw_s, rw_r, rwl_sem, rz_s, rz_r,
):
    b = lax.axis_index("batch")
    m = lax.axis_index("member")
    t = lax.axis_index("tensor")
    y, x = m // 4, m % 4

    def z_dev(d):
        return (b, m, (t + d) % 4)

    def plane_dev(dy, dx):
        return (b, ((y + dy) % 4) * 4 + (x + dx) % 4, t)

    other = (1 - b, m, t)

    def remote(src, dst, s, r, dev):
        return pltpu.make_async_remote_copy(
            src_ref=src, dst_ref=dst, send_sem=s, recv_sem=r, device_id=dev, device_id_type=MESH
        )

    started = []

    def go(copy):
        copy.start()
        started.append(copy)

    def al(v, k):
        return pl.multiple_of(v, k)

    def quarter(q):
        return pl.ds(al((q % 4) * FQ, 128), FQ)

    mine_cols = pl.ds(al(b * FH, 128), FH)
    other_cols = pl.ds(al((1 - b) * FH, 128), FH)

    barrier = pltpu.get_barrier_semaphore()
    for d in range(1, 4):
        pl.semaphore_signal(barrier, inc=1, device_id=z_dev(d), device_id_type=MESH)
    pl.semaphore_signal(barrier, inc=1, device_id=other, device_id_type=MESH)

    for dy, dx in ((0, 1), (0, 3), (1, 0), (3, 0)):
        pl.semaphore_signal(barrier, inc=1, device_id=plane_dev(dy, dx), device_id_type=MESH)

    own_rows = rows.at[pl.ds(al(t * 16, 16), 16), pl.ds(0, F)]
    load_rows = pltpu.make_async_copy(rows_hbm, own_rows, loc_sem.at[0])
    load_target = pltpu.make_async_copy(
        target_hbm, rows.at[pl.ds(0, 64), pl.ds(F, FQ)], loc_sem.at[1]
    )
    load_w_in = pltpu.make_async_copy(w_in_hbm.at[0], w_in, loc_sem.at[2])
    load_w_out = pltpu.make_async_copy(w_out_hbm.at[0], w_out, loc_sem.at[3])
    load_rows.start()
    load_target.start()
    load_w_in.start()
    load_w_out.start()
    pl.semaphore_wait(barrier, 3 + 1 + 4)

    load_rows.wait()
    for d in (2, 1, 3):
        go(remote(own_rows, own_rows, zg_s.at[d - 1], zg_r.at[d - 1], z_dev(d)))
    load_target.wait()
    for d in (1, 3, 2):
        theirs = rows.at[pl.ds(al(((t + 4 - d) % 4) * 16, 16), 16), pl.ds(0, F)]
        remote(own_rows, theirs, zg_s.at[d - 1], zg_r.at[d - 1], z_dev(d)).wait_recv()

    def hop(k):
        _, first, skip, n, land, (dy, dx) = HOPS[k]
        return remote(
            rows.at[pl.ds(POS[first] + skip, n)],
            rows.at[pl.ds(POS[land] + skip, n)],
            xy_s.at[k],
            xy_r.at[k],
            plane_dev(dy, dx),
        )

    here = set()

    def arrived(names):
        for name in names:
            if name not in here:
                here.add(name)
                for k in range(len(HOPS)):
                    if HOPS[k][0] == name:
                        hop(k).wait_recv()

    def send_hops(names):
        for name in names:
            for k in range(len(HOPS)):
                if HOPS[k][0] == name:
                    go(hop(k))

    def core_copy(kind, c):
        r = pl.ds(OFF[c], SIZE[c])
        if kind == 0:
            src, dst = rows.at[r, other_cols], rows_o.at[r]
        else:
            src, dst = hid.at[0, r], hid.at[1, r]
        return remote(src, dst, core_s.at[kind, c], core_r.at[kind, c], other)

    def forward(c):
        arrived(NEEDS[c])
        if c == 0:
            load_w_in.wait()
        r = pl.ds(OFF[c], SIZE[c])
        go(core_copy(0, c))

        @pl.loop(0, HS // 256, unroll=True)
        def _(n):
            cols = pl.ds(al(n * 256, 256), 256)
            v = dot(rows[r, pl.ds(0, F)], w_in[:, cols])
            s = jax.nn.sigmoid(v)
            hid[0, r, cols] = (v * s).astype(BF16)
            slope[r, cols] = s * (1.0 + v * (1.0 - s))

        go(core_copy(1, c))

    def halves(c, way):
        h = SIZE[c] // 2
        return pl.ds(OFF[c] + way * h, h), pl.ds(OFF[c] // 2, h)

    def predict(c, rel):
        r = pl.ds(OFF[c], SIZE[c])
        part[rel, r] = dot(hid[0, r], w_out[:, quarter(t + rel)])

    def predict_first(c):
        if c == 0:
            load_w_out.wait()
        for way, rel in ((0, 3), (1, 1)):
            predict(c, rel)
            r, q = halves(c, way)
            sbuf[0, way, q] = part[rel, r].astype(BF16)
            go(rs(c, 0, way))

    def rs(c, s, way):
        _, q = halves(c, way)
        return remote(
            sbuf.at[s, way, q], rbuf.at[s, way, q], rs_s.at[c, s, way], rs_r.at[c, s, way],
            z_dev(1 + 2 * way),
        )

    def rs_step(c, s):
        for way in range(2):
            rs(c, s - 1, way).wait_recv()
            rel = (3 - s) if way == 0 else (1 + s)
            r, q = halves(c, way)
            sbuf[s, way, q] = (part[rel, r] + rbuf[s - 1, way, q].astype(F32)).astype(BF16)
            go(rs(c, s, way))

    def ag_copy(c, k, way, incoming):
        r, _ = halves(c, way if k != 1 else 1 - way)
        source = t if k < 2 else t + 3 - 2 * way
        if incoming:
            source = source + 3 - 2 * way
        ref = err.at[r, quarter(source)]
        return remote(ref, ref, ag_s.at[c, k, way], ag_r.at[c, k, way], z_dev(1 + 2 * way))

    def errors(c):
        for way in range(2):
            rs(c, 2, way).wait_recv()
            r, q = halves(c, way)
            pred = part[0, r] + rbuf[2, way, q].astype(F32)
            goal = rows[r, pl.ds(F, FQ)].astype(F32)
            err[r, quarter(t)] = ((pred - goal) * SCALE).astype(BF16)
            pred_b[r] = pred.astype(BF16)
            go(ag_copy(c, 0, way, False))
        for way in range(2):
            go(ag_copy(c, 1, way, False))

    def ag_forward(c):
        for way in range(2):
            ag_copy(c, 0, way, True).wait_recv()
            go(ag_copy(c, 2, way, False))

    def reward_send(c):
        for strip in CHUNKS[c]:
            half, dy, dx = int(strip[0] == "B"), int(strip[1]), int(strip[2])
            k = POS[strip] // ST
            src = pred_b.at[pl.ds(POS[strip], ST)]
            dst = gathered.at[m, pl.ds(ST * half, ST)]
            if (dy, dx) == (0, 0):
                pltpu.make_async_copy(src, dst, rwl_sem.at[half]).start()
            else:
                go(remote(src, dst, rw_s.at[k], rw_r.at[m, half], plane_dev(dy, dx)))

    def group_rows(g):
        c0, c1 = GROUPS[g][0], GROUPS[g][-1]
        return pl.ds(OFF[c0], OFF[c1] + SIZE[c1] - OFF[c0])

    def group_copy(kind, g):
        r = group_rows(g)
        if kind == 0:
            src, dst = err.at[r, other_cols], err_o.at[r]
        else:
            src, dst = pre.at[0, r], pre.at[1, r]
        return remote(src, dst, grp_s.at[kind, g], grp_r.at[kind, g], other)

    def back(g):
        for c in GROUPS[g]:
            for k in (1, 2):
                for way in range(2):
                    ag_copy(c, k, way, True).wait_recv()
        go(group_copy(0, g))
        r = group_rows(g)

        @pl.loop(0, HS // 256, unroll=True)
        def _(n):
            cols = pl.ds(al(n * 256, 256), 256)
            v = dot_nt(err[r], w_out[cols, :])
            pre[0, r, cols] = (v * slope[r, cols]).astype(BF16)

        go(group_copy(1, g))

    begun = set()

    def grad_out(g):
        for c in GROUPS[g]:
            core_copy(1, c).wait_recv()
        group_copy(0, g).wait_recv()
        r = group_rows(g)
        first = "out" not in begun
        begun.add("out")

        @pl.loop(0, HS // 256, unroll=True)
        def _(n):
            cols = pl.ds(al(n * 256, 256), 256)
            v = dot_tn(hid[0, r, cols], err[r, mine_cols]) + dot_tn(hid[1, r, cols], err_o[r])
            acc_out[0, cols, :] = v if first else acc_out[0, cols, :] + v

    def grad_in(g):
        for c in GROUPS[g]:
            core_copy(0, c).wait_recv()
        group_copy(1, g).wait_recv()
        r = group_rows(g)
        first = "in" not in begun
        begun.add("in")

        @pl.loop(0, FH // 256, unroll=True)
        def _(n):
            mine = pl.ds(al(b * FH + n * 256, 128), 256)
            cols = pl.ds(al(n * 256, 256), 256)
            v = dot_tn(rows[r, mine], pre[0, r]) + dot_tn(rows_o[r, cols], pre[1, r])
            acc_in[0, cols, :] = v if first else acc_in[0, cols, :] + v

    def spread_copy(d):
        return remote(
            spread.at[pl.ds(al(((t + d) % 4) * 16, 16), 16)],
            spread_r.at[d - 1],
            rz_s.at[d - 1],
            rz_r.at[d - 1],
            z_dev(d),
        )

    def reward_first():
        @pl.loop(1, MEMBERS)
        def _(d):
            s = (m + d) % MEMBERS
            for half in range(2):
                remote(
                    pred_b.at[pl.ds(0, ST)],
                    gathered.at[s, pl.ds(ST * half, ST)],
                    rw_s.at[2],
                    rw_r.at[s, half],
                    (b, s, t),
                ).wait_recv()

        for half in range(2):
            pltpu.make_async_copy(
                pred_b.at[pl.ds(ST * half, ST)],
                gathered.at[m, pl.ds(ST * half, ST)],
                rwl_sem.at[half],
            ).wait()

        total = jnp.zeros((64, 128), F32)
        for k in range(3):
            cols = pl.ds(128 * k, 128)
            mean = jnp.zeros((64, 128), F32)
            for s in range(MEMBERS):
                mean += gathered[s, :, cols].astype(F32)
            mean = mean * (1.0 / MEMBERS)
            for s in range(MEMBERS):
                dev = gathered[s, :, cols].astype(F32) - mean
                total += dev * dev
        spread[...] = total
        for d in range(1, 4):
            go(spread_copy(d))

    def reward_last():
        for d in range(1, 4):
            spread_copy(d).wait_recv()
        own = spread[pl.ds(al(t * 16, 16), 16)]
        for d in range(3):
            own += spread_r[d]
        reward_ref[...] = jnp.sum(own.T, axis=0, keepdims=True) * (1.0 / (MEMBERS * F))

    def sent(keep):
        while len(started) > keep:
            started.pop(0).wait_send()

    for step in ORDER:
        kind, k = step[0], int(step[1:])
        if kind == "P":
            send_hops(("p1", "p2"))
        elif kind == "X":
            arrived(RELAY[step][0])
            send_hops(RELAY[step][1])
        elif kind == "F":
            forward(k)
        elif kind == "G":
            predict_first(k)
        elif kind == "H":
            predict(k, 2)
            predict(k, 0)
        elif kind == "R":
            rs_step(k, 1)
        elif kind == "S":
            rs_step(k, 2)
        elif kind == "E":
            errors(k)
        elif kind == "A":
            ag_forward(k)
        elif kind == "W":
            reward_send(k)
        elif kind == "B":
            back(k)
        elif kind == "O":
            grad_out(k)
        elif kind == "I":
            grad_in(k)
        elif kind == "T":
            sent(16)
        elif step == "Y1":
            reward_first()
        else:
            reward_last()
    sent(0)


def per_device(rows_in, target, w_in, w_out):
    any_spec = pl.BlockSpec(memory_space=pl.ANY)
    vmem = pltpu.VMEM
    dma = pltpu.SemaphoreType.DMA
    reward, grad_in, grad_out = pl.pallas_call(
        kernel,
        out_shape=(
            vmem((1, 16), F32),
            vmem((1, FH, HS), F32),
            vmem((1, HS, FH), F32),
        ),
        in_specs=[any_spec] * 4,
        out_specs=(pl.BlockSpec(memory_space=pltpu.VMEM),) * 3,
        scratch_shapes=[
            vmem((F, HS), BF16),
            vmem((HS, F), BF16),
            vmem((R, W), BF16),
            vmem((R, FH), BF16),
            vmem((2, R, HS), BF16),
            vmem((R, HS), F32),
            vmem((4, R, FQ), F32),
            vmem((3, 2, R // 2, FQ), BF16),
            vmem((3, 2, R // 2, FQ), BF16),
            vmem((R, F), BF16),
            vmem((R, FH), BF16),
            vmem((2, R, HS), BF16),
            vmem((R, FQ), BF16),
            vmem((MEMBERS, 64, FQ), BF16),
            vmem((64, 128), F32),
            vmem((3, 16, 128), F32),
            dma((4,)),
            dma((3,)),
            dma((3,)),
            dma((len(HOPS),)),
            dma((len(HOPS),)),
            dma((NC, 3, 2)),
            dma((NC, 3, 2)),
            dma((NC, 3, 2)),
            dma((NC, 3, 2)),
            dma((2, NC)),
            dma((2, NC)),
            dma((2, NG)),
            dma((2, NG)),
            dma((len(STRIPS),)),
            dma((MEMBERS, 2)),
            dma((2,)),
            dma((3,)),
            dma((3,)),
        ],
        compiler_params=pltpu.CompilerParams(
            collective_id=0, has_side_effects=True, vmem_limit_bytes=54 * 1024 * 1024
        ),
        name="ensemble",
    )(rows_in, target, w_in, w_out)
    return reward.reshape(16), grad_in, grad_out


def solution(mesh):
    return jax.shard_map(
        per_device,
        mesh=mesh,
        in_specs=(
            P(("batch", "member", "tensor"), None),
            P(("batch", "member"), "tensor"),
            P("member", None, "tensor"),
            P("member", "tensor", None),
        ),
        out_specs=(
            P(("batch", "member", "tensor")),
            P("member", "batch", "tensor"),
            P("member", "tensor", "batch"),
        ),
        check_vma=False,
    )
```

```python
import jax
import jax.numpy as jnp
from jax import lax
from jax.experimental import pallas as pl
from jax.experimental.pallas import tpu as pltpu
from jax.sharding import PartitionSpec as P

MESH = pl.DeviceIdType.MESH
F32 = jnp.float32
BF16 = jnp.bfloat16

F = 1536
FH = F // 2
FQ = F // 4
HS = 1024
R = 1024
W = F + FQ
ST = 32
MEMBERS = 16
SCALE = 2048.0**-0.5

CHUNKS = (
    ("A00", "B00"),
    ("A01", "A03", "B10", "B30"),
    ("A10", "A30", "B01", "B03"),
    ("A11", "A13", "A31", "A33", "B11", "B31", "B13", "B33"),
    ("A02", "A12", "A32", "B20", "B21", "B23"),
    ("A20", "A23", "B02", "B32"),
    ("A21", "A22", "B12", "B22"),
)
STRIPS = tuple(s for chunk in CHUNKS for s in chunk)
POS = {s: ST * k for k, s in enumerate(STRIPS)}
SIZE = tuple(ST * len(chunk) for chunk in CHUNKS)
OFF = tuple(sum(SIZE[:c]) for c in range(len(CHUNKS)))
NC = len(CHUNKS)
GROUPS = ((0, 1, 2), (3,), (4,), (5, 6))
NG = len(GROUPS)
LAST = GROUPS[-1]
LB = OFF[LAST[0]]
LN = R - LB

HOPS = (
    ("p1", "A00", 0, 32, "A03", (0, 1)),
    ("p1", "A00", 0, 32, "A01", (0, 3)),
    ("p1", "B00", 0, 32, "B30", (1, 0)),
    ("p1", "B00", 0, 32, "B10", (3, 0)),
    ("p2", "A00", 0, 32, "A30", (1, 0)),
    ("p2", "A00", 0, 32, "A10", (3, 0)),
    ("p2", "B00", 0, 32, "B03", (0, 1)),
    ("p2", "B00", 0, 32, "B01", (0, 3)),
    ("d", "A03", 0, 16, "A02", (0, 1)),
    ("d", "A01", 16, 16, "A02", (0, 3)),
    ("d", "B30", 0, 16, "B20", (1, 0)),
    ("d", "B10", 16, 16, "B20", (3, 0)),
    ("q3", "A01", 0, 64, "A31", (1, 0)),
    ("q3", "A01", 0, 64, "A11", (3, 0)),
    ("q3", "B10", 0, 64, "B13", (0, 1)),
    ("q3", "B10", 0, 64, "B11", (0, 3)),
    ("q4", "A02", 0, 32, "A32", (1, 0)),
    ("q4", "A02", 0, 32, "A12", (3, 0)),
    ("q4", "B20", 0, 32, "B23", (0, 1)),
    ("q4", "B20", 0, 32, "B21", (0, 3)),
    ("q5", "A33", 0, 32, "A23", (1, 0)),
    ("q5", "A10", 0, 32, "A20", (3, 0)),
    ("q5", "B33", 0, 32, "B32", (0, 1)),
    ("q5", "B01", 0, 32, "B02", (0, 3)),
    ("q6", "A32", 0, 32, "A22", (1, 0)),
    ("q6", "A11", 0, 32, "A21", (3, 0)),
    ("q6", "B23", 0, 32, "B22", (0, 1)),
    ("q6", "B11", 0, 32, "B12", (0, 3)),
)
NEEDS = ((), ("p1",), ("p2",), ("q3",), ("d", "q4"), ("q5",), ("q6",))
RELAY = {
    "X1": (("p1",), ("d", "q3")),
    "X2": (("d",), ("q4",)),
    "X3": (("p2", "q3"), ("q5",)),
    "X4": (("q3", "q4"), ("q6",)),
}
ORDER = (
    "P1", "F0", "G0", "H0", "R0", "X1", "F1", "G1", "S0", "F2", "G2", "H2", "H1", "R1", "X2",
    "E0", "R2", "S1", "A0", "F3", "S2", "X3", "G3", "E1", "F4", "E2", "G4", "H3", "F5", "X4",
    "H5", "H4", "G5", "W0", "W1", "R3", "A2", "R4", "F6", "A1", "H6", "S3", "G6", "W2", "S4",
    "R5", "T3", "B0", "E3", "R6", "A3", "W3", "S5", "T3", "I0", "S6", "E4", "W4", "O0", "E5",
    "W5", "E6", "W6", "T3", "B1", "A4", "A5", "O1", "A6", "I1", "T2", "B2", "Y1", "B3", "O2",
    "I2", "Y2", "Z1",
)


def dot(a, b):
    return lax.dot_general(a, b, (((1,), (0,)), ((), ())), preferred_element_type=F32)


def dot_nt(a, b):
    return lax.dot_general(a, b, (((1,), (1,)), ((), ())), preferred_element_type=F32)


def dot_tn(a, b):
    return lax.dot_general(a, b, (((0,), (0,)), ((), ())), preferred_element_type=F32)


def kernel(
    rows_hbm, target_hbm, w_in_hbm, w_out_hbm,
    reward_ref, acc_in, acc_out, hid_l, pre_l, err_l, rows_l,
    w_in, w_out, rows, rows_o, hid, slope, part, sbuf, rbuf, err, err_o, pre,
    pred_b, gathered, spread, spread_r,
    loc_sem, zg_s, zg_r, xy_s, xy_r, rs_s, rs_r, ag_s, ag_r, core_s, core_r, grp_s, grp_r,
    rw_s, rw_r, rwl_sem, rz_s, rz_r,
):
    b = lax.axis_index("batch")
    m = lax.axis_index("member")
    t = lax.axis_index("tensor")
    y, x = m // 4, m % 4

    def z_dev(d):
        return (b, m, (t + d) % 4)

    def plane_dev(dy, dx):
        return (b, ((y + dy) % 4) * 4 + (x + dx) % 4, t)

    other = (1 - b, m, t)

    def remote(src, dst, s, r, dev):
        return pltpu.make_async_remote_copy(
            src_ref=src, dst_ref=dst, send_sem=s, recv_sem=r, device_id=dev, device_id_type=MESH
        )

    started = []

    def go(copy):
        copy.start()
        started.append(copy)

    def al(v, k):
        return pl.multiple_of(v, k)

    def quarter(q):
        return pl.ds(al((q % 4) * FQ, 128), FQ)

    mine_cols = pl.ds(al(b * FH, 128), FH)
    other_cols = pl.ds(al((1 - b) * FH, 128), FH)

    barrier = pltpu.get_barrier_semaphore()
    for d in range(1, 4):
        pl.semaphore_signal(barrier, inc=1, device_id=z_dev(d), device_id_type=MESH)
    pl.semaphore_signal(barrier, inc=1, device_id=other, device_id_type=MESH)

    for dy, dx in ((0, 1), (0, 3), (1, 0), (3, 0)):
        pl.semaphore_signal(barrier, inc=1, device_id=plane_dev(dy, dx), device_id_type=MESH)

    own_rows = rows.at[pl.ds(al(t * 16, 16), 16), pl.ds(0, F)]
    load_rows = pltpu.make_async_copy(rows_hbm, own_rows, loc_sem.at[0])
    load_target = pltpu.make_async_copy(
        target_hbm, rows.at[pl.ds(0, 64), pl.ds(F, FQ)], loc_sem.at[1]
    )
    load_w_in = pltpu.make_async_copy(w_in_hbm.at[0], w_in, loc_sem.at[2])
    load_w_out = pltpu.make_async_copy(w_out_hbm.at[0], w_out, loc_sem.at[3])
    load_rows.start()
    load_target.start()
    load_w_in.start()
    load_w_out.start()
    pl.semaphore_wait(barrier, 3 + 1 + 4)

    load_rows.wait()
    for d in (2, 1, 3):
        go(remote(own_rows, own_rows, zg_s.at[d - 1], zg_r.at[d - 1], z_dev(d)))
    load_target.wait()
    for d in (1, 3, 2):
        theirs = rows.at[pl.ds(al(((t + 4 - d) % 4) * 16, 16), 16), pl.ds(0, F)]
        remote(own_rows, theirs, zg_s.at[d - 1], zg_r.at[d - 1], z_dev(d)).wait_recv()

    def hop(k):
        _, first, skip, n, land, (dy, dx) = HOPS[k]
        return remote(
            rows.at[pl.ds(POS[first] + skip, n)],
            rows.at[pl.ds(POS[land] + skip, n)],
            xy_s.at[k],
            xy_r.at[k],
            plane_dev(dy, dx),
        )

    here = set()

    def arrived(names):
        for name in names:
            if name not in here:
                here.add(name)
                for k in range(len(HOPS)):
                    if HOPS[k][0] == name:
                        hop(k).wait_recv()

    def send_hops(names):
        for name in names:
            for k in range(len(HOPS)):
                if HOPS[k][0] == name:
                    go(hop(k))

    def hid_of(whose, c):
        if c in LAST:
            return hid_l.at[whose, pl.ds(OFF[c] - LB, SIZE[c])]
        return hid.at[whose, pl.ds(OFF[c], SIZE[c])]

    def core_copy(kind, c):
        r = pl.ds(OFF[c], SIZE[c])
        if kind == 1:
            src, dst = hid_of(0, c), hid_of(1, c)
        elif c in LAST:
            src, dst = rows.at[r, other_cols], rows_l.at[1, pl.ds(OFF[c] - LB, SIZE[c])]
        else:
            src, dst = rows.at[r, other_cols], rows_o.at[r]
        return remote(src, dst, core_s.at[kind, c], core_r.at[kind, c], other)

    def forward(c):
        arrived(NEEDS[c])
        if c == 0:
            load_w_in.wait()
        r = pl.ds(OFF[c], SIZE[c])
        go(core_copy(0, c))
        out = hid_of(0, c)

        @pl.loop(0, HS // 256, unroll=True)
        def _(n):
            cols = pl.ds(al(n * 256, 256), 256)
            v = dot(rows[r, pl.ds(0, F)], w_in[:, cols])
            s = jax.nn.sigmoid(v)
            out[:, cols] = (v * s).astype(BF16)
            slope[r, cols] = s * (1.0 + v * (1.0 - s))

        go(core_copy(1, c))

    def halves(c, way):
        h = SIZE[c] // 2
        return pl.ds(OFF[c] + way * h, h), pl.ds(OFF[c] // 2, h)

    def predict(c, rel):
        r = pl.ds(OFF[c], SIZE[c])
        part[rel, r] = dot(hid_of(0, c)[...], w_out[:, quarter(t + rel)])

    def predict_first(c):
        if c == 0:
            load_w_out.wait()
        for way, rel in ((0, 3), (1, 1)):
            predict(c, rel)
            r, q = halves(c, way)
            sbuf[0, way, q] = part[rel, r].astype(BF16)
            go(rs(c, 0, way))

    def rs(c, s, way):
        _, q = halves(c, way)
        return remote(
            sbuf.at[s, way, q], rbuf.at[s, way, q], rs_s.at[c, s, way], rs_r.at[c, s, way],
            z_dev(1 + 2 * way),
        )

    def rs_step(c, s):
        for way in range(2):
            rs(c, s - 1, way).wait_recv()
            rel = (3 - s) if way == 0 else (1 + s)
            r, q = halves(c, way)
            sbuf[s, way, q] = (part[rel, r] + rbuf[s - 1, way, q].astype(F32)).astype(BF16)
            go(rs(c, s, way))

    def ag_copy(c, k, way, incoming):
        r, _ = halves(c, way if k != 1 else 1 - way)
        source = t if k < 2 else t + 3 - 2 * way
        if incoming:
            source = source + 3 - 2 * way
        ref = err.at[r, quarter(source)]
        return remote(ref, ref, ag_s.at[c, k, way], ag_r.at[c, k, way], z_dev(1 + 2 * way))

    def errors(c):
        for way in range(2):
            rs(c, 2, way).wait_recv()
            r, q = halves(c, way)
            pred = part[0, r] + rbuf[2, way, q].astype(F32)
            goal = rows[r, pl.ds(F, FQ)].astype(F32)
            err[r, quarter(t)] = ((pred - goal) * SCALE).astype(BF16)
            pred_b[r] = pred.astype(BF16)
            go(ag_copy(c, 0, way, False))
        for way in range(2):
            go(ag_copy(c, 1, way, False))

    def ag_forward(c):
        for way in range(2):
            ag_copy(c, 0, way, True).wait_recv()
            go(ag_copy(c, 2, way, False))

    def reward_send(c):
        for strip in CHUNKS[c]:
            half, dy, dx = int(strip[0] == "B"), int(strip[1]), int(strip[2])
            k = POS[strip] // ST
            src = pred_b.at[pl.ds(POS[strip], ST)]
            dst = gathered.at[m, pl.ds(ST * half, ST)]
            if (dy, dx) == (0, 0):
                pltpu.make_async_copy(src, dst, rwl_sem.at[half]).start()
            else:
                go(remote(src, dst, rw_s.at[k], rw_r.at[m, half], plane_dev(dy, dx)))

    def group_rows(g):
        c0, c1 = GROUPS[g][0], GROUPS[g][-1]
        return pl.ds(OFF[c0], OFF[c1] + SIZE[c1] - OFF[c0])

    def group_copy(kind, g):
        r = group_rows(g)
        last = g == NG - 1
        if kind == 0:
            src, dst = err.at[r, other_cols], err_l.at[1] if last else err_o.at[r]
        elif last:
            src, dst = pre_l.at[0], pre_l.at[1]
        else:
            src, dst = pre.at[0, r], pre.at[1, r]
        return remote(src, dst, grp_s.at[kind, g], grp_r.at[kind, g], other)

    def back(g):
        for c in GROUPS[g]:
            for k in (1, 2):
                for way in range(2):
                    ag_copy(c, k, way, True).wait_recv()
        go(group_copy(0, g))
        r = group_rows(g)
        out = pre_l.at[0] if g == NG - 1 else pre.at[0, r]

        @pl.loop(0, HS // 256, unroll=True)
        def _(n):
            cols = pl.ds(al(n * 256, 256), 256)
            v = dot_nt(err[r], w_out[cols, :])
            out[:, cols] = (v * slope[r, cols]).astype(BF16)

        go(group_copy(1, g))
        if g == NG - 1:
            err_l[0] = err[r, mine_cols]
            rows_l[0] = rows[r, mine_cols]

    def last_arrived():
        for c in LAST:
            core_copy(0, c).wait_recv()
            core_copy(1, c).wait_recv()
        group_copy(0, NG - 1).wait_recv()
        group_copy(1, NG - 1).wait_recv()

    begun = set()

    def grad_out(g):
        for c in GROUPS[g]:
            core_copy(1, c).wait_recv()
        group_copy(0, g).wait_recv()
        r = group_rows(g)
        first = "out" not in begun
        begun.add("out")

        @pl.loop(0, HS // 256, unroll=True)
        def _(n):
            cols = pl.ds(al(n * 256, 256), 256)
            v = dot_tn(hid[0, r, cols], err[r, mine_cols]) + dot_tn(hid[1, r, cols], err_o[r])
            acc_out[cols, :] = v if first else acc_out[cols, :] + v

    def grad_in(g):
        for c in GROUPS[g]:
            core_copy(0, c).wait_recv()
        group_copy(1, g).wait_recv()
        r = group_rows(g)
        first = "in" not in begun
        begun.add("in")

        @pl.loop(0, FH // 256, unroll=True)
        def _(n):
            mine = pl.ds(al(b * FH + n * 256, 128), 256)
            cols = pl.ds(al(n * 256, 256), 256)
            v = dot_tn(rows[r, mine], pre[0, r]) + dot_tn(rows_o[r, cols], pre[1, r])
            acc_in[cols, :] = v if first else acc_in[cols, :] + v

    def spread_copy(d):
        return remote(
            spread.at[pl.ds(al(((t + d) % 4) * 16, 16), 16)],
            spread_r.at[d - 1],
            rz_s.at[d - 1],
            rz_r.at[d - 1],
            z_dev(d),
        )

    def reward_first():
        @pl.loop(1, MEMBERS)
        def _(d):
            s = (m + d) % MEMBERS
            for half in range(2):
                remote(
                    pred_b.at[pl.ds(0, ST)],
                    gathered.at[s, pl.ds(ST * half, ST)],
                    rw_s.at[2],
                    rw_r.at[s, half],
                    (b, s, t),
                ).wait_recv()

        for half in range(2):
            pltpu.make_async_copy(
                pred_b.at[pl.ds(ST * half, ST)],
                gathered.at[m, pl.ds(ST * half, ST)],
                rwl_sem.at[half],
            ).wait()

        total = jnp.zeros((64, 128), F32)
        for k in range(3):
            cols = pl.ds(128 * k, 128)
            mean = jnp.zeros((64, 128), F32)
            for s in range(MEMBERS):
                mean += gathered[s, :, cols].astype(F32)
            mean = mean * (1.0 / MEMBERS)
            for s in range(MEMBERS):
                dev = gathered[s, :, cols].astype(F32) - mean
                total += dev * dev
        spread[...] = total
        for d in range(1, 4):
            go(spread_copy(d))

    def reward_last():
        for d in range(1, 4):
            spread_copy(d).wait_recv()
        own = spread[pl.ds(al(t * 16, 16), 16)]
        for d in range(3):
            own += spread_r[d]
        reward_ref[...] = jnp.sum(own.T, axis=0, keepdims=True) * (1.0 / (MEMBERS * F))

    def sent(keep):
        while len(started) > keep:
            started.pop(0).wait_send()

    for step in ORDER:
        kind, k = step[0], int(step[1:])
        if kind == "P":
            send_hops(("p1", "p2"))
        elif kind == "X":
            arrived(RELAY[step][0])
            send_hops(RELAY[step][1])
        elif kind == "F":
            forward(k)
        elif kind == "G":
            predict_first(k)
        elif kind == "H":
            predict(k, 2)
            predict(k, 0)
        elif kind == "R":
            rs_step(k, 1)
        elif kind == "S":
            rs_step(k, 2)
        elif kind == "E":
            errors(k)
        elif kind == "A":
            ag_forward(k)
        elif kind == "W":
            reward_send(k)
        elif kind == "B":
            back(k)
        elif kind == "O":
            grad_out(k)
        elif kind == "I":
            grad_in(k)
        elif kind == "T":
            sent(10 * k)
        elif kind == "Z":
            last_arrived()
        elif step == "Y1":
            reward_first()
        else:
            reward_last()
    sent(0)


def finish(
    reward, acc_in, acc_out, hid_l, pre_l, err_l, rows_l,
    reward_ref, grad_in_hbm, grad_out_hbm, tile_in, tile_out, sem,
):
    reward_ref[...] = reward[...]
    copies = []
    for n in range(HS // 256):
        cols = pl.ds(n * 256, 256)
        v = dot_tn(hid_l[0, :, cols], err_l[0]) + dot_tn(hid_l[1, :, cols], err_l[1])
        tile_out[cols, :] = acc_out[cols, :] + v
        copies.append(
            pltpu.make_async_copy(tile_out.at[cols], grad_out_hbm.at[0, cols], sem.at[n])
        )
        copies[-1].start()
    for n in range(FH // 256):
        cols = pl.ds(n * 256, 256)
        v = dot_tn(rows_l[0, :, cols], pre_l[0]) + dot_tn(rows_l[1, :, cols], pre_l[1])
        tile_in[cols, :] = acc_in[cols, :] + v
        copies.append(
            pltpu.make_async_copy(tile_in.at[cols], grad_in_hbm.at[0, cols], sem.at[4 + n])
        )
        copies[-1].start()
    for copy in copies:
        copy.wait()


def per_device(rows_in, target, w_in, w_out):
    any_spec = pl.BlockSpec(memory_space=pl.ANY)
    vmem_spec = pl.BlockSpec(memory_space=pltpu.VMEM)
    vmem = pltpu.VMEM
    dma = pltpu.SemaphoreType.DMA
    parts = pl.pallas_call(
        kernel,
        out_shape=(
            vmem((1, 16), F32),
            vmem((FH, HS), F32),
            vmem((HS, FH), F32),
            vmem((2, LN, HS), BF16),
            vmem((2, LN, HS), BF16),
            vmem((2, LN, FH), BF16),
            vmem((2, LN, FH), BF16),
        ),
        in_specs=[any_spec] * 4,
        out_specs=(vmem_spec,) * 7,
        scratch_shapes=[
            vmem((F, HS), BF16),
            vmem((HS, F), BF16),
            vmem((R, W), BF16),
            vmem((LB, FH), BF16),
            vmem((2, LB, HS), BF16),
            vmem((R, HS), F32),
            vmem((4, R, FQ), F32),
            vmem((3, 2, R // 2, FQ), BF16),
            vmem((3, 2, R // 2, FQ), BF16),
            vmem((R, F), BF16),
            vmem((LB, FH), BF16),
            vmem((2, LB, HS), BF16),
            vmem((R, FQ), BF16),
            vmem((MEMBERS, 64, FQ), BF16),
            vmem((64, 128), F32),
            vmem((3, 16, 128), F32),
            dma((4,)),
            dma((3,)),
            dma((3,)),
            dma((len(HOPS),)),
            dma((len(HOPS),)),
            dma((NC, 3, 2)),
            dma((NC, 3, 2)),
            dma((NC, 3, 2)),
            dma((NC, 3, 2)),
            dma((2, NC)),
            dma((2, NC)),
            dma((2, NG)),
            dma((2, NG)),
            dma((len(STRIPS),)),
            dma((MEMBERS, 2)),
            dma((2,)),
            dma((3,)),
            dma((3,)),
        ],
        compiler_params=pltpu.CompilerParams(
            collective_id=0, has_side_effects=True, vmem_limit_bytes=46 * 1024 * 1024
        ),
        name="ensemble",
    )(rows_in, target, w_in, w_out)
    reward, grad_in, grad_out = pl.pallas_call(
        finish,
        out_shape=(
            jax.ShapeDtypeStruct((1, 16), F32),
            jax.ShapeDtypeStruct((1, FH, HS), F32),
            jax.ShapeDtypeStruct((1, HS, FH), F32),
        ),
        in_specs=[vmem_spec] * 7,
        out_specs=(vmem_spec, any_spec, any_spec),
        scratch_shapes=[vmem((FH, HS), F32), vmem((HS, FH), F32), dma((7,))],
        compiler_params=pltpu.CompilerParams(vmem_limit_bytes=24 * 1024 * 1024),
        name="finish",
    )(*parts)
    return reward.reshape(16), grad_in, grad_out


def solution(mesh):
    return jax.shard_map(
        per_device,
        mesh=mesh,
        in_specs=(
            P(("batch", "member", "tensor"), None),
            P(("batch", "member"), "tensor"),
            P("member", None, "tensor"),
            P("member", "tensor", None),
        ),
        out_specs=(
            P(("batch", "member", "tensor")),
            P("member", "batch", "tensor"),
            P("member", "tensor", "batch"),
        ),
        check_vma=False,
    )
```

```python
import jax
import jax.numpy as jnp
from jax import lax
from jax.experimental import pallas as pl
from jax.experimental.pallas import tpu as pltpu
from jax.sharding import PartitionSpec as P

MESH = pl.DeviceIdType.MESH
F32 = jnp.float32
BF16 = jnp.bfloat16

F = 1536
FH = F // 2
FQ = F // 4
HS = 1024
R = 1024
ST = 32
MEMBERS = 16
SCALE = 2048.0**-0.5

CHUNKS = (
    ("A00", "B00"),
    ("A01", "A03", "B10", "B30"),
    ("A10", "A30", "B01", "B03"),
    ("A11", "A13", "A31", "A33", "B11", "B31", "B13", "B33"),
    ("A02", "A12", "A32", "B20", "B21", "B23"),
    ("A20", "A23", "B02", "B32"),
    ("A21", "A22", "B12", "B22"),
)
STRIPS = tuple(s for chunk in CHUNKS for s in chunk)
POS = {s: ST * k for k, s in enumerate(STRIPS)}
SIZE = tuple(ST * len(chunk) for chunk in CHUNKS)
OFF = tuple(sum(SIZE[:c]) for c in range(len(CHUNKS)))
NC = len(CHUNKS)
GROUPS = ((0, 1, 2), (3,), (4,), (5, 6))
NG = len(GROUPS)
LAST = GROUPS[-1]
LB = OFF[LAST[0]]
LN = R - LB

HOPS = (
    ("p1", "A00", 0, 32, "A03", (0, 1)),
    ("p1", "A00", 0, 32, "A01", (0, 3)),
    ("p1", "B00", 0, 32, "B30", (1, 0)),
    ("p1", "B00", 0, 32, "B10", (3, 0)),
    ("p2", "A00", 0, 32, "A30", (1, 0)),
    ("p2", "A00", 0, 32, "A10", (3, 0)),
    ("p2", "B00", 0, 32, "B03", (0, 1)),
    ("p2", "B00", 0, 32, "B01", (0, 3)),
    ("d", "A03", 0, 16, "A02", (0, 1)),
    ("d", "A01", 16, 16, "A02", (0, 3)),
    ("d", "B30", 0, 16, "B20", (1, 0)),
    ("d", "B10", 16, 16, "B20", (3, 0)),
    ("q3", "A01", 0, 64, "A31", (1, 0)),
    ("q3", "A01", 0, 64, "A11", (3, 0)),
    ("q3", "B10", 0, 64, "B13", (0, 1)),
    ("q3", "B10", 0, 64, "B11", (0, 3)),
    ("q4", "A02", 0, 32, "A32", (1, 0)),
    ("q4", "A02", 0, 32, "A12", (3, 0)),
    ("q4", "B20", 0, 32, "B23", (0, 1)),
    ("q4", "B20", 0, 32, "B21", (0, 3)),
    ("q5", "A33", 0, 32, "A23", (1, 0)),
    ("q5", "A10", 0, 32, "A20", (3, 0)),
    ("q5", "B33", 0, 32, "B32", (0, 1)),
    ("q5", "B01", 0, 32, "B02", (0, 3)),
    ("q6", "A32", 0, 32, "A22", (1, 0)),
    ("q6", "A11", 0, 32, "A21", (3, 0)),
    ("q6", "B23", 0, 32, "B22", (0, 1)),
    ("q6", "B11", 0, 32, "B12", (0, 3)),
)
HOPS += tuple((h[0].upper(),) + h[1:] for h in HOPS)
GOALS = ((), ("P1",), ("P2",), ("Q3",), ("D", "Q4"), ("Q5",), ("Q6",))
NEEDS = ((), ("p1",), ("p2",), ("q3",), ("d", "q4"), ("q5",), ("q6",))
RELAY = {
    "X1": (("p1",), ("d", "q3")),
    "X2": (("d",), ("q4",)),
    "X3": (("p2", "q3"), ("q5",)),
    "X4": (("q3", "q4"), ("q6",)),
    "X5": ((), ("P1", "P2")),
    "X6": (("P1",), ("D", "Q3")),
    "X7": (("D", "P2", "Q3"), ("Q4", "Q5")),
    "X8": (("Q4",), ("Q6",)),
}
ORDER = (
    "P1", "F0", "G0", "H0", "R0", "X1", "X5", "F1", "G1", "S0", "F2", "G2", "H2", "H1", "R1",
    "X2", "E0", "R2", "S1", "A0", "F3", "S2", "X3", "G3", "E1", "X6", "F4", "E2", "G4", "H3",
    "F5", "X4", "H5", "H4", "G5", "W0", "W1", "R3", "A2", "X7", "R4", "F6", "A1", "H6", "S3",
    "X8", "G6", "W2", "S4", "R5", "T3", "B0", "E3", "R6", "A3", "W3", "S5", "T3", "I0", "S6",
    "E4", "W4", "O0", "E5", "W5", "E6", "W6", "T3", "B1", "A4", "A5", "O1", "A6", "I1", "T2",
    "B2", "Y1", "B3", "O2", "I2", "Y2", "Z1",
)


def dot(a, b):
    return lax.dot_general(a, b, (((1,), (0,)), ((), ())), preferred_element_type=F32)


def dot_nt(a, b):
    return lax.dot_general(a, b, (((1,), (1,)), ((), ())), preferred_element_type=F32)


def dot_tn(a, b):
    return lax.dot_general(a, b, (((0,), (0,)), ((), ())), preferred_element_type=F32)


def kernel(
    rows_hbm, target_hbm, w_in_hbm, w_out_hbm,
    reward_ref, acc_in, acc_out, hid_l, pre_l, err_l, rows_l,
    w_in, w_out, rows, goal, rows_o, hid, slope, part, sbuf, rbuf, err, err_o, pre,
    pred_b, gathered, spread, spread_r,
    loc_sem, zg_s, zg_r, xy_s, xy_r, rs_s, rs_r, ag_s, ag_r, core_s, core_r, grp_s, grp_r,
    rw_s, rw_r, rwl_sem, rz_s, rz_r,
):
    b = lax.axis_index("batch")
    m = lax.axis_index("member")
    t = lax.axis_index("tensor")
    y, x = m // 4, m % 4

    def z_dev(d):
        return (b, m, (t + d) % 4)

    def plane_dev(dy, dx):
        return (b, ((y + dy) % 4) * 4 + (x + dx) % 4, t)

    other = (1 - b, m, t)

    def remote(src, dst, s, r, dev):
        return pltpu.make_async_remote_copy(
            src_ref=src, dst_ref=dst, send_sem=s, recv_sem=r, device_id=dev, device_id_type=MESH
        )

    started = []

    def go(copy):
        copy.start()
        started.append(copy)

    def al(v, k):
        return pl.multiple_of(v, k)

    def quarter(q):
        return pl.ds(al((q % 4) * FQ, 128), FQ)

    mine_cols = pl.ds(al(b * FH, 128), FH)
    other_cols = pl.ds(al((1 - b) * FH, 128), FH)

    barrier = pltpu.get_barrier_semaphore()
    for d in range(1, 4):
        pl.semaphore_signal(barrier, inc=1, device_id=z_dev(d), device_id_type=MESH)
    pl.semaphore_signal(barrier, inc=1, device_id=other, device_id_type=MESH)

    for dy, dx in ((0, 1), (0, 3), (1, 0), (3, 0)):
        pl.semaphore_signal(barrier, inc=1, device_id=plane_dev(dy, dx), device_id_type=MESH)

    own_rows = rows.at[pl.ds(al(t * 16, 16), 16)]
    load_rows = pltpu.make_async_copy(rows_hbm, own_rows, loc_sem.at[0])
    load_target = pltpu.make_async_copy(
        target_hbm, goal.at[pl.ds(0, 64)], loc_sem.at[1]
    )
    load_w_in = pltpu.make_async_copy(w_in_hbm.at[0], w_in, loc_sem.at[2])
    load_w_out = pltpu.make_async_copy(w_out_hbm.at[0], w_out, loc_sem.at[3])
    load_rows.start()
    load_target.start()
    load_w_in.start()
    load_w_out.start()
    pl.semaphore_wait(barrier, 3 + 1 + 4)

    load_rows.wait()
    for d in (2, 1, 3):
        go(remote(own_rows, own_rows, zg_s.at[d - 1], zg_r.at[d - 1], z_dev(d)))
    for d in (1, 3, 2):
        theirs = rows.at[pl.ds(al(((t + 4 - d) % 4) * 16, 16), 16)]
        remote(own_rows, theirs, zg_s.at[d - 1], zg_r.at[d - 1], z_dev(d)).wait_recv()

    def hop(k):
        name, first, skip, n, land, (dy, dx) = HOPS[k]
        of = goal if name.isupper() else rows
        return remote(
            of.at[pl.ds(POS[first] + skip, n)],
            of.at[pl.ds(POS[land] + skip, n)],
            xy_s.at[k],
            xy_r.at[k],
            plane_dev(dy, dx),
        )

    here = set()

    def arrived(names):
        for name in names:
            if name not in here:
                here.add(name)
                for k in range(len(HOPS)):
                    if HOPS[k][0] == name:
                        hop(k).wait_recv()

    def send_hops(names):
        for name in names:
            for k in range(len(HOPS)):
                if HOPS[k][0] == name:
                    go(hop(k))

    def hid_of(whose, c):
        if c in LAST:
            return hid_l.at[whose, pl.ds(OFF[c] - LB, SIZE[c])]
        return hid.at[whose, pl.ds(OFF[c], SIZE[c])]

    def core_copy(kind, c):
        r = pl.ds(OFF[c], SIZE[c])
        if kind == 1:
            src, dst = hid_of(0, c), hid_of(1, c)
        elif c in LAST:
            src, dst = rows.at[r, other_cols], rows_l.at[1, pl.ds(OFF[c] - LB, SIZE[c])]
        else:
            src, dst = rows.at[r, other_cols], rows_o.at[r]
        return remote(src, dst, core_s.at[kind, c], core_r.at[kind, c], other)

    def forward(c):
        arrived(NEEDS[c])
        if c == 0:
            load_w_in.wait()
        r = pl.ds(OFF[c], SIZE[c])
        go(core_copy(0, c))
        out = hid_of(0, c)

        @pl.loop(0, HS // 256, unroll=True)
        def _(n):
            cols = pl.ds(al(n * 256, 256), 256)
            v = dot(rows[r], w_in[:, cols])
            s = jax.nn.sigmoid(v)
            out[:, cols] = (v * s).astype(BF16)
            slope[r, cols] = s * (1.0 + v * (1.0 - s))

        go(core_copy(1, c))

    def halves(c, way):
        h = SIZE[c] // 2
        return pl.ds(OFF[c] + way * h, h), pl.ds(OFF[c] // 2, h)

    def predict(c, rel):
        r = pl.ds(OFF[c], SIZE[c])
        part[rel, r] = dot(hid_of(0, c)[...], w_out[:, quarter(t + rel)])

    def predict_first(c):
        if c == 0:
            load_w_out.wait()
        for way, rel in ((0, 3), (1, 1)):
            predict(c, rel)
            r, q = halves(c, way)
            sbuf[0, way, q] = part[rel, r].astype(BF16)
            go(rs(c, 0, way))

    def rs(c, s, way):
        _, q = halves(c, way)
        return remote(
            sbuf.at[s, way, q], rbuf.at[s, way, q], rs_s.at[c, s, way], rs_r.at[c, s, way],
            z_dev(1 + 2 * way),
        )

    def rs_step(c, s):
        for way in range(2):
            rs(c, s - 1, way).wait_recv()
            rel = (3 - s) if way == 0 else (1 + s)
            r, q = halves(c, way)
            sbuf[s, way, q] = (part[rel, r] + rbuf[s - 1, way, q].astype(F32)).astype(BF16)
            go(rs(c, s, way))

    def ag_copy(c, k, way, incoming):
        r, _ = halves(c, way if k != 1 else 1 - way)
        source = t if k < 2 else t + 3 - 2 * way
        if incoming:
            source = source + 3 - 2 * way
        ref = err.at[r, quarter(source)]
        return remote(ref, ref, ag_s.at[c, k, way], ag_r.at[c, k, way], z_dev(1 + 2 * way))

    def errors(c):
        arrived(GOALS[c])
        for way in range(2):
            rs(c, 2, way).wait_recv()
            r, q = halves(c, way)
            pred = part[0, r] + rbuf[2, way, q].astype(F32)
            err[r, quarter(t)] = ((pred - goal[r].astype(F32)) * SCALE).astype(BF16)
            pred_b[r] = pred.astype(BF16)
            go(ag_copy(c, 0, way, False))
        for way in range(2):
            go(ag_copy(c, 1, way, False))

    def ag_forward(c):
        for way in range(2):
            ag_copy(c, 0, way, True).wait_recv()
            go(ag_copy(c, 2, way, False))

    def reward_send(c):
        for strip in CHUNKS[c]:
            half, dy, dx = int(strip[0] == "B"), int(strip[1]), int(strip[2])
            k = POS[strip] // ST
            src = pred_b.at[pl.ds(POS[strip], ST)]
            dst = gathered.at[m, pl.ds(ST * half, ST)]
            if (dy, dx) == (0, 0):
                pltpu.make_async_copy(src, dst, rwl_sem.at[half]).start()
            else:
                go(remote(src, dst, rw_s.at[k], rw_r.at[m, half], plane_dev(dy, dx)))

    def group_rows(g):
        c0, c1 = GROUPS[g][0], GROUPS[g][-1]
        return pl.ds(OFF[c0], OFF[c1] + SIZE[c1] - OFF[c0])

    def group_copy(kind, g):
        r = group_rows(g)
        last = g == NG - 1
        if kind == 0:
            src, dst = err.at[r, other_cols], err_l.at[1] if last else err_o.at[r]
        elif last:
            src, dst = pre_l.at[0], pre_l.at[1]
        else:
            src, dst = pre.at[0, r], pre.at[1, r]
        return remote(src, dst, grp_s.at[kind, g], grp_r.at[kind, g], other)

    def back(g):
        for c in GROUPS[g]:
            for k in (1, 2):
                for way in range(2):
                    ag_copy(c, k, way, True).wait_recv()
        go(group_copy(0, g))
        r = group_rows(g)
        out = pre_l.at[0] if g == NG - 1 else pre.at[0, r]

        @pl.loop(0, HS // 256, unroll=True)
        def _(n):
            cols = pl.ds(al(n * 256, 256), 256)
            v = dot_nt(err[r], w_out[cols, :])
            out[:, cols] = (v * slope[r, cols]).astype(BF16)

        go(group_copy(1, g))
        if g == NG - 1:
            err_l[0] = err[r, mine_cols]
            rows_l[0] = rows[r, mine_cols]

    def last_arrived():
        for c in LAST:
            core_copy(0, c).wait_recv()
            core_copy(1, c).wait_recv()
        group_copy(0, NG - 1).wait_recv()
        group_copy(1, NG - 1).wait_recv()

    begun = set()

    def grad_out(g):
        for c in GROUPS[g]:
            core_copy(1, c).wait_recv()
        group_copy(0, g).wait_recv()
        r = group_rows(g)
        first = "out" not in begun
        begun.add("out")

        @pl.loop(0, HS // 256, unroll=True)
        def _(n):
            cols = pl.ds(al(n * 256, 256), 256)
            v = dot_tn(hid[0, r, cols], err[r, mine_cols]) + dot_tn(hid[1, r, cols], err_o[r])
            acc_out[cols, :] = v if first else acc_out[cols, :] + v

    def grad_in(g):
        for c in GROUPS[g]:
            core_copy(0, c).wait_recv()
        group_copy(1, g).wait_recv()
        r = group_rows(g)
        first = "in" not in begun
        begun.add("in")

        @pl.loop(0, FH // 256, unroll=True)
        def _(n):
            mine = pl.ds(al(b * FH + n * 256, 128), 256)
            cols = pl.ds(al(n * 256, 256), 256)
            v = dot_tn(rows[r, mine], pre[0, r]) + dot_tn(rows_o[r, cols], pre[1, r])
            acc_in[cols, :] = v if first else acc_in[cols, :] + v

    def spread_copy(d):
        return remote(
            spread.at[pl.ds(al(((t + d) % 4) * 16, 16), 16)],
            spread_r.at[d - 1],
            rz_s.at[d - 1],
            rz_r.at[d - 1],
            z_dev(d),
        )

    def reward_first():
        @pl.loop(1, MEMBERS)
        def _(d):
            s = (m + d) % MEMBERS
            for half in range(2):
                remote(
                    pred_b.at[pl.ds(0, ST)],
                    gathered.at[s, pl.ds(ST * half, ST)],
                    rw_s.at[2],
                    rw_r.at[s, half],
                    (b, s, t),
                ).wait_recv()

        for half in range(2):
            pltpu.make_async_copy(
                pred_b.at[pl.ds(ST * half, ST)],
                gathered.at[m, pl.ds(ST * half, ST)],
                rwl_sem.at[half],
            ).wait()

        total = jnp.zeros((64, 128), F32)
        for k in range(3):
            cols = pl.ds(128 * k, 128)
            mean = jnp.zeros((64, 128), F32)
            for s in range(MEMBERS):
                mean += gathered[s, :, cols].astype(F32)
            mean = mean * (1.0 / MEMBERS)
            for s in range(MEMBERS):
                dev = gathered[s, :, cols].astype(F32) - mean
                total += dev * dev
        spread[...] = total
        for d in range(1, 4):
            go(spread_copy(d))

    def reward_last():
        for d in range(1, 4):
            spread_copy(d).wait_recv()
        own = spread[pl.ds(al(t * 16, 16), 16)]
        for d in range(3):
            own += spread_r[d]
        reward_ref[...] = jnp.sum(own.T, axis=0, keepdims=True) * (1.0 / (MEMBERS * F))

    def sent(keep):
        while len(started) > keep:
            started.pop(0).wait_send()

    for step in ORDER:
        kind, k = step[0], int(step[1:])
        if kind == "P":
            send_hops(("p1", "p2"))
        elif kind == "X":
            if step == "X5":
                load_target.wait()
            arrived(RELAY[step][0])
            send_hops(RELAY[step][1])
        elif kind == "F":
            forward(k)
        elif kind == "G":
            predict_first(k)
        elif kind == "H":
            predict(k, 2)
            predict(k, 0)
        elif kind == "R":
            rs_step(k, 1)
        elif kind == "S":
            rs_step(k, 2)
        elif kind == "E":
            errors(k)
        elif kind == "A":
            ag_forward(k)
        elif kind == "W":
            reward_send(k)
        elif kind == "B":
            back(k)
        elif kind == "O":
            grad_out(k)
        elif kind == "I":
            grad_in(k)
        elif kind == "T":
            sent(10 * k)
        elif kind == "Z":
            last_arrived()
        elif step == "Y1":
            reward_first()
        else:
            reward_last()
    sent(0)


def finish(
    reward, acc_in, acc_out, hid_l, pre_l, err_l, rows_l,
    reward_ref, grad_in_hbm, grad_out_hbm, tile_in, tile_out, sem,
):
    reward_ref[...] = reward[...]
    copies = []
    for n in range(HS // 256):
        cols = pl.ds(n * 256, 256)
        v = dot_tn(hid_l[0, :, cols], err_l[0]) + dot_tn(hid_l[1, :, cols], err_l[1])
        tile_out[cols, :] = acc_out[cols, :] + v
        copies.append(
            pltpu.make_async_copy(tile_out.at[cols], grad_out_hbm.at[0, cols], sem.at[n])
        )
        copies[-1].start()
    for n in range(FH // 256):
        cols = pl.ds(n * 256, 256)
        v = dot_tn(rows_l[0, :, cols], pre_l[0]) + dot_tn(rows_l[1, :, cols], pre_l[1])
        tile_in[cols, :] = acc_in[cols, :] + v
        copies.append(
            pltpu.make_async_copy(tile_in.at[cols], grad_in_hbm.at[0, cols], sem.at[4 + n])
        )
        copies[-1].start()
    for copy in copies:
        copy.wait()


def per_device(rows_in, target, w_in, w_out):
    any_spec = pl.BlockSpec(memory_space=pl.ANY)
    vmem_spec = pl.BlockSpec(memory_space=pltpu.VMEM)
    vmem = pltpu.VMEM
    dma = pltpu.SemaphoreType.DMA
    parts = pl.pallas_call(
        kernel,
        out_shape=(
            vmem((1, 16), F32),
            vmem((FH, HS), F32),
            vmem((HS, FH), F32),
            vmem((2, LN, HS), BF16),
            vmem((2, LN, HS), BF16),
            vmem((2, LN, FH), BF16),
            vmem((2, LN, FH), BF16),
        ),
        in_specs=[any_spec] * 4,
        out_specs=(vmem_spec,) * 7,
        scratch_shapes=[
            vmem((F, HS), BF16),
            vmem((HS, F), BF16),
            vmem((R, F), BF16),
            vmem((R, FQ), BF16),
            vmem((LB, FH), BF16),
            vmem((2, LB, HS), BF16),
            vmem((R, HS), F32),
            vmem((4, R, FQ), F32),
            vmem((3, 2, R // 2, FQ), BF16),
            vmem((3, 2, R // 2, FQ), BF16),
            vmem((R, F), BF16),
            vmem((LB, FH), BF16),
            vmem((2, LB, HS), BF16),
            vmem((R, FQ), BF16),
            vmem((MEMBERS, 64, FQ), BF16),
            vmem((64, 128), F32),
            vmem((3, 16, 128), F32),
            dma((4,)),
            dma((3,)),
            dma((3,)),
            dma((len(HOPS),)),
            dma((len(HOPS),)),
            dma((NC, 3, 2)),
            dma((NC, 3, 2)),
            dma((NC, 3, 2)),
            dma((NC, 3, 2)),
            dma((2, NC)),
            dma((2, NC)),
            dma((2, NG)),
            dma((2, NG)),
            dma((len(STRIPS),)),
            dma((MEMBERS, 2)),
            dma((2,)),
            dma((3,)),
            dma((3,)),
        ],
        compiler_params=pltpu.CompilerParams(
            collective_id=0, has_side_effects=True, vmem_limit_bytes=46 * 1024 * 1024
        ),
        name="ensemble",
    )(rows_in, target, w_in, w_out)
    reward, grad_in, grad_out = pl.pallas_call(
        finish,
        out_shape=(
            jax.ShapeDtypeStruct((1, 16), F32),
            jax.ShapeDtypeStruct((1, FH, HS), F32),
            jax.ShapeDtypeStruct((1, HS, FH), F32),
        ),
        in_specs=[vmem_spec] * 7,
        out_specs=(vmem_spec, any_spec, any_spec),
        scratch_shapes=[vmem((FH, HS), F32), vmem((HS, FH), F32), dma((7,))],
        compiler_params=pltpu.CompilerParams(vmem_limit_bytes=24 * 1024 * 1024),
        name="finish",
    )(*parts)
    return reward.reshape(16), grad_in, grad_out


def solution(mesh):
    return jax.shard_map(
        per_device,
        mesh=mesh,
        in_specs=(
            P(("batch", "member", "tensor"), None),
            P(("batch", "member"), "tensor"),
            P("member", None, "tensor"),
            P("member", "tensor", None),
        ),
        out_specs=(
            P(("batch", "member", "tensor")),
            P("member", "batch", "tensor"),
            P("member", "tensor", "batch"),
        ),
        check_vma=False,
    )
```

```python
import jax
import jax.numpy as jnp
from jax import lax
from jax.experimental import pallas as pl
from jax.experimental.pallas import tpu as pltpu
from jax.sharding import PartitionSpec as P

MESH = pl.DeviceIdType.MESH
F32 = jnp.float32
BF16 = jnp.bfloat16

F = 1536
FH = F // 2
FQ = F // 4
HS = 1024
R = 1024
ST = 32
MEMBERS = 16
SCALE = 2048.0**-0.5

CHUNKS = (
    ("A00", "B00"),
    ("A01", "A03", "B10", "B30"),
    ("A10", "A30", "B01", "B03"),
    ("A11", "A13", "A31", "A33", "B11", "B31", "B13", "B33"),
    ("A02", "A12", "A32", "B20", "B21", "B23"),
    ("A20", "A23", "B02", "B32"),
    ("A21", "A22", "B12", "B22"),
)
STRIPS = tuple(s for chunk in CHUNKS for s in chunk)
POS = {s: ST * k for k, s in enumerate(STRIPS)}
SIZE = tuple(ST * len(chunk) for chunk in CHUNKS)
OFF = tuple(sum(SIZE[:c]) for c in range(len(CHUNKS)))
NC = len(CHUNKS)
GROUPS = ((0, 1, 2), (3,), (4,), (5, 6))
NG = len(GROUPS)
LAST = GROUPS[-1]
LB = OFF[LAST[0]]
LN = R - LB

HOPS = (
    ("p1", "A00", 0, 32, "A03", (0, 1)),
    ("p1", "A00", 0, 32, "A01", (0, 3)),
    ("p1", "B00", 0, 32, "B30", (1, 0)),
    ("p1", "B00", 0, 32, "B10", (3, 0)),
    ("p2", "A00", 0, 32, "A30", (1, 0)),
    ("p2", "A00", 0, 32, "A10", (3, 0)),
    ("p2", "B00", 0, 32, "B03", (0, 1)),
    ("p2", "B00", 0, 32, "B01", (0, 3)),
    ("d", "A03", 0, 16, "A02", (0, 1)),
    ("d", "A01", 16, 16, "A02", (0, 3)),
    ("d", "B30", 0, 16, "B20", (1, 0)),
    ("d", "B10", 16, 16, "B20", (3, 0)),
    ("q3", "A01", 0, 64, "A31", (1, 0)),
    ("q3", "A01", 0, 64, "A11", (3, 0)),
    ("q3", "B10", 0, 64, "B13", (0, 1)),
    ("q3", "B10", 0, 64, "B11", (0, 3)),
    ("q4", "A02", 0, 32, "A32", (1, 0)),
    ("q4", "A02", 0, 32, "A12", (3, 0)),
    ("q4", "B20", 0, 32, "B23", (0, 1)),
    ("q4", "B20", 0, 32, "B21", (0, 3)),
    ("q5", "A33", 0, 32, "A23", (1, 0)),
    ("q5", "A10", 0, 32, "A20", (3, 0)),
    ("q5", "B33", 0, 32, "B32", (0, 1)),
    ("q5", "B01", 0, 32, "B02", (0, 3)),
    ("q6", "A32", 0, 32, "A22", (1, 0)),
    ("q6", "A11", 0, 32, "A21", (3, 0)),
    ("q6", "B23", 0, 32, "B22", (0, 1)),
    ("q6", "B11", 0, 32, "B12", (0, 3)),
)
HOPS += tuple((h[0].upper(),) + h[1:] for h in HOPS)
GOALS = ((), ("P1",), ("P2",), ("Q3",), ("D", "Q4"), ("Q5",), ("Q6",))
NEEDS = ((), ("p1",), ("p2",), ("q3",), ("d", "q4"), ("q5",), ("q6",))
RELAY = {
    "X1": (("p1",), ("d", "q3")),
    "X2": (("d",), ("q4",)),
    "X3": (("p2", "q3"), ("q5",)),
    "X4": (("q3", "q4"), ("q6",)),
    "X5": ((), ("P1", "P2")),
    "X6": (("P1",), ("D", "Q3")),
    "X7": (("D", "P2", "Q3"), ("Q4", "Q5")),
    "X8": (("Q4",), ("Q6",)),
}
ORDER = (
    "P1", "F0", "G0", "H0", "R0", "X1", "X5", "F1", "G1", "S0", "F2", "G2", "H2", "H1", "R1",
    "X2", "E0", "R2", "S1", "A0", "F3", "S2", "X3", "G3", "E1", "X6", "F4", "E2", "G4", "H3",
    "F5", "X4", "H5", "H4", "G5", "W0", "W1", "R3", "A2", "X7", "R4", "F6", "A1", "H6", "S3",
    "X8", "G6", "W2", "S4", "R5", "T3", "B0", "E3", "R6", "A3", "W3", "S5", "T3", "I0", "S6",
    "E4", "W4", "O0", "E5", "W5", "E6", "W6", "T3", "B1", "A4", "A5", "O1", "A6", "I1", "T2",
    "B2", "Y1", "B3", "O2", "I2", "Y2", "Z1",
)


def dot(a, b):
    return lax.dot_general(a, b, (((1,), (0,)), ((), ())), preferred_element_type=F32)


def dot_nt(a, b):
    return lax.dot_general(a, b, (((1,), (1,)), ((), ())), preferred_element_type=F32)


def dot_tn(a, b):
    return lax.dot_general(a, b, (((0,), (0,)), ((), ())), preferred_element_type=F32)


def kernel(
    rows_hbm, target_hbm, w_in_hbm, w_out_hbm,
    reward_ref, acc_in, acc_out, hid_l, pre_l, err_l, rows_l,
    w_in, w_out, rows, goal, rows_o, hid, slope, part, sbuf, rbuf, err, err_o, pre,
    pred_b, gathered, spread, spread_r,
    loc_sem, zg_s, zg_r, xy_s, xy_r, rs_s, rs_r, ag_s, ag_r, core_s, core_r, grp_s, grp_r,
    rw_s, rw_r, rwl_sem, rz_s, rz_r,
):
    b = lax.axis_index("batch")
    m = lax.axis_index("member")
    t = lax.axis_index("tensor")
    y, x = m // 4, m % 4

    def z_dev(d):
        return (b, m, (t + d) % 4)

    def plane_dev(dy, dx):
        return (b, ((y + dy) % 4) * 4 + (x + dx) % 4, t)

    other = (1 - b, m, t)

    def remote(src, dst, s, r, dev):
        return pltpu.make_async_remote_copy(
            src_ref=src, dst_ref=dst, send_sem=s, recv_sem=r, device_id=dev, device_id_type=MESH
        )

    started = []

    def go(copy):
        copy.start()
        started.append(copy)

    def al(v, k):
        return pl.multiple_of(v, k)

    def quarter(q):
        return pl.ds(al((q % 4) * FQ, 128), FQ)

    mine_cols = pl.ds(al(b * FH, 128), FH)
    other_cols = pl.ds(al((1 - b) * FH, 128), FH)

    barrier = pltpu.get_barrier_semaphore()
    for d in range(1, 4):
        pl.semaphore_signal(barrier, inc=1, device_id=z_dev(d), device_id_type=MESH)
    pl.semaphore_signal(barrier, inc=1, device_id=other, device_id_type=MESH)

    for dy, dx in ((0, 1), (0, 3), (1, 0), (3, 0)):
        pl.semaphore_signal(barrier, inc=1, device_id=plane_dev(dy, dx), device_id_type=MESH)

    own_rows = rows.at[pl.ds(al(t * 16, 16), 16)]
    load_rows = pltpu.make_async_copy(rows_hbm, own_rows, loc_sem.at[0])
    load_target = pltpu.make_async_copy(
        target_hbm, goal.at[pl.ds(0, 64)], loc_sem.at[1]
    )
    load_w_in = pltpu.make_async_copy(w_in_hbm.at[0], w_in, loc_sem.at[2])
    load_w_out = pltpu.make_async_copy(w_out_hbm.at[0], w_out, loc_sem.at[3])
    load_rows.start()
    load_target.start()
    load_w_in.start()
    load_w_out.start()
    pl.semaphore_wait(barrier, 3 + 1 + 4)

    load_rows.wait()
    for d in (2, 1, 3):
        go(remote(own_rows, own_rows, zg_s.at[d - 1], zg_r.at[d - 1], z_dev(d)))
    for d in (1, 3, 2):
        theirs = rows.at[pl.ds(al(((t + 4 - d) % 4) * 16, 16), 16)]
        remote(own_rows, theirs, zg_s.at[d - 1], zg_r.at[d - 1], z_dev(d)).wait_recv()

    def hop(k):
        name, first, skip, n, land, (dy, dx) = HOPS[k]
        of = goal if name.isupper() else rows
        return remote(
            of.at[pl.ds(POS[first] + skip, n)],
            of.at[pl.ds(POS[land] + skip, n)],
            xy_s.at[k],
            xy_r.at[k],
            plane_dev(dy, dx),
        )

    here = set()

    def arrived(names):
        for name in names:
            if name not in here:
                here.add(name)
                for k in range(len(HOPS)):
                    if HOPS[k][0] == name:
                        hop(k).wait_recv()

    def send_hops(names):
        for name in names:
            for k in range(len(HOPS)):
                if HOPS[k][0] == name:
                    go(hop(k))

    def hid_of(whose, c):
        if c in LAST:
            return hid_l.at[whose, pl.ds(OFF[c] - LB, SIZE[c])]
        return hid.at[whose, pl.ds(OFF[c], SIZE[c])]

    def core_copy(kind, c):
        r = pl.ds(OFF[c], SIZE[c])
        if kind == 1:
            src, dst = hid_of(0, c), hid_of(1, c)
        elif c in LAST:
            src, dst = rows.at[r, other_cols], rows_l.at[1, pl.ds(OFF[c] - LB, SIZE[c])]
        else:
            src, dst = rows.at[r, other_cols], rows_o.at[r]
        return remote(src, dst, core_s.at[kind, c], core_r.at[kind, c], other)

    def forward(c):
        arrived(NEEDS[c])
        if c == 0:
            load_w_in.wait()
        r = pl.ds(OFF[c], SIZE[c])
        go(core_copy(0, c))
        out = hid_of(0, c)

        @pl.loop(0, HS // 256, unroll=True)
        def _(n):
            cols = pl.ds(al(n * 256, 256), 256)
            v = dot(rows[r], w_in[:, cols])
            s = jax.nn.sigmoid(v)
            out[:, cols] = (v * s).astype(BF16)
            slope[r, cols] = s * (1.0 + v * (1.0 - s))

        go(core_copy(1, c))

    def halves(c, way):
        h = SIZE[c] // 2
        return pl.ds(OFF[c] + way * h, h), pl.ds(OFF[c] // 2, h)

    def predict(c, rel):
        r = pl.ds(OFF[c], SIZE[c])
        part[rel, r] = dot(hid_of(0, c)[...], w_out[:, quarter(t + rel)])

    def predict_first(c):
        if c == 0:
            load_w_out.wait()
        for way, rel in ((0, 3), (1, 1)):
            predict(c, rel)
            r, q = halves(c, way)
            sbuf[0, way, q] = part[rel, r].astype(BF16)
            go(rs(c, 0, way))

    def rs(c, s, way):
        _, q = halves(c, way)
        return remote(
            sbuf.at[s, way, q], rbuf.at[s, way, q], rs_s.at[c, s, way], rs_r.at[c, s, way],
            z_dev(1 + 2 * way),
        )

    def rs_step(c, s):
        for way in range(2):
            rs(c, s - 1, way).wait_recv()
            rel = (3 - s) if way == 0 else (1 + s)
            r, q = halves(c, way)
            sbuf[s, way, q] = (part[rel, r] + rbuf[s - 1, way, q].astype(F32)).astype(BF16)
            go(rs(c, s, way))

    def ag_copy(c, k, way, incoming):
        r, _ = halves(c, way if k != 1 else 1 - way)
        source = t if k < 2 else t + 3 - 2 * way
        if incoming:
            source = source + 3 - 2 * way
        ref = err.at[r, quarter(source)]
        return remote(ref, ref, ag_s.at[c, k, way], ag_r.at[c, k, way], z_dev(1 + 2 * way))

    def errors(c):
        arrived(GOALS[c])
        for way in range(2):
            rs(c, 2, way).wait_recv()
            r, q = halves(c, way)
            pred = part[0, r] + rbuf[2, way, q].astype(F32)
            err[r, quarter(t)] = ((pred - goal[r].astype(F32)) * SCALE).astype(BF16)
            pred_b[r] = pred.astype(BF16)
            go(ag_copy(c, 0, way, False))
        for way in range(2):
            go(ag_copy(c, 1, way, False))

    def ag_forward(c):
        for way in range(2):
            ag_copy(c, 0, way, True).wait_recv()
            go(ag_copy(c, 2, way, False))

    def reward_send(c):
        for strip in CHUNKS[c]:
            half, dy, dx = int(strip[0] == "B"), int(strip[1]), int(strip[2])
            k = POS[strip] // ST
            src = pred_b.at[pl.ds(POS[strip], ST)]
            dst = gathered.at[m, pl.ds(ST * half, ST)]
            if (dy, dx) == (0, 0):
                pltpu.make_async_copy(src, dst, rwl_sem.at[half]).start()
            else:
                go(remote(src, dst, rw_s.at[k], rw_r.at[m, half], plane_dev(dy, dx)))

    def group_rows(g):
        c0, c1 = GROUPS[g][0], GROUPS[g][-1]
        return pl.ds(OFF[c0], OFF[c1] + SIZE[c1] - OFF[c0])

    def group_copy(kind, g):
        r = group_rows(g)
        last = g == NG - 1
        if kind == 0:
            src, dst = err.at[r, other_cols], err_l.at[1] if last else err_o.at[r]
        elif last:
            src, dst = pre_l.at[0], pre_l.at[1]
        else:
            src, dst = pre.at[0, r], pre.at[1, r]
        return remote(src, dst, grp_s.at[kind, g], grp_r.at[kind, g], other)

    def back(g):
        for c in GROUPS[g]:
            for k in (1, 2):
                for way in range(2):
                    ag_copy(c, k, way, True).wait_recv()
        go(group_copy(0, g))
        r = group_rows(g)
        out = pre_l.at[0] if g == NG - 1 else pre.at[0, r]

        @pl.loop(0, HS // 256, unroll=True)
        def _(n):
            cols = pl.ds(al(n * 256, 256), 256)
            v = dot_nt(err[r], w_out[cols, :])
            out[:, cols] = (v * slope[r, cols]).astype(BF16)

        go(group_copy(1, g))
        if g == NG - 1:
            err_l[0] = err[r, mine_cols]
            rows_l[0] = rows[r, mine_cols]

    def last_arrived():
        for c in LAST:
            core_copy(0, c).wait_recv()
            core_copy(1, c).wait_recv()
        group_copy(0, NG - 1).wait_recv()
        group_copy(1, NG - 1).wait_recv()

    begun = set()

    def grad_out(g):
        for c in GROUPS[g]:
            core_copy(1, c).wait_recv()
        group_copy(0, g).wait_recv()
        r = group_rows(g)
        first = "out" not in begun
        begun.add("out")

        @pl.loop(0, HS // 256, unroll=True)
        def _(n):
            cols = pl.ds(al(n * 256, 256), 256)
            v = dot_tn(hid[0, r, cols], err[r, mine_cols]) + dot_tn(hid[1, r, cols], err_o[r])
            acc_out[cols, :] = v if first else acc_out[cols, :] + v

    def grad_in(g):
        for c in GROUPS[g]:
            core_copy(0, c).wait_recv()
        group_copy(1, g).wait_recv()
        r = group_rows(g)
        first = "in" not in begun
        begun.add("in")

        @pl.loop(0, FH // 256, unroll=True)
        def _(n):
            mine = pl.ds(al(b * FH + n * 256, 128), 256)
            cols = pl.ds(al(n * 256, 256), 256)
            v = dot_tn(rows[r, mine], pre[0, r]) + dot_tn(rows_o[r, cols], pre[1, r])
            acc_in[cols, :] = v if first else acc_in[cols, :] + v

    def spread_copy(d):
        return remote(
            spread.at[pl.ds(al(((t + d) % 4) * 16, 16), 16)],
            spread_r.at[d - 1],
            rz_s.at[d - 1],
            rz_r.at[d - 1],
            z_dev(d),
        )

    def reward_first():
        @pl.loop(1, MEMBERS)
        def _(d):
            s = (m + d) % MEMBERS
            for half in range(2):
                remote(
                    pred_b.at[pl.ds(0, ST)],
                    gathered.at[s, pl.ds(ST * half, ST)],
                    rw_s.at[2],
                    rw_r.at[s, half],
                    (b, s, t),
                ).wait_recv()

        for half in range(2):
            pltpu.make_async_copy(
                pred_b.at[pl.ds(ST * half, ST)],
                gathered.at[m, pl.ds(ST * half, ST)],
                rwl_sem.at[half],
            ).wait()

        total = jnp.zeros((64, 128), F32)
        for k in range(3):
            cols = pl.ds(128 * k, 128)
            mean = jnp.zeros((64, 128), F32)
            for s in range(MEMBERS):
                mean += gathered[s, :, cols].astype(F32)
            mean = mean * (1.0 / MEMBERS)
            for s in range(MEMBERS):
                dev = gathered[s, :, cols].astype(F32) - mean
                total += dev * dev
        spread[...] = total
        for d in range(1, 4):
            go(spread_copy(d))

    def reward_last():
        for d in range(1, 4):
            spread_copy(d).wait_recv()
        own = spread[pl.ds(al(t * 16, 16), 16)]
        for d in range(3):
            own += spread_r[d]
        reward_ref[...] = jnp.sum(own.T, axis=0, keepdims=True) * (1.0 / (MEMBERS * F))

    def sent(keep):
        while len(started) > keep:
            started.pop(0).wait_send()

    for step in ORDER:
        kind, k = step[0], int(step[1:])
        if kind == "P":
            send_hops(("p1", "p2"))
        elif kind == "X":
            if step == "X5":
                load_target.wait()
            arrived(RELAY[step][0])
            send_hops(RELAY[step][1])
        elif kind == "F":
            forward(k)
        elif kind == "G":
            predict_first(k)
        elif kind == "H":
            predict(k, 2)
            predict(k, 0)
        elif kind == "R":
            rs_step(k, 1)
        elif kind == "S":
            rs_step(k, 2)
        elif kind == "E":
            errors(k)
        elif kind == "A":
            ag_forward(k)
        elif kind == "W":
            reward_send(k)
        elif kind == "B":
            back(k)
        elif kind == "O":
            grad_out(k)
        elif kind == "I":
            grad_in(k)
        elif kind == "T":
            sent(10 * k)
        elif kind == "Z":
            last_arrived()
        elif step == "Y1":
            reward_first()
        else:
            reward_last()
    sent(0)


def finish(
    reward, acc_in, acc_out, hid_l, pre_l, err_l, rows_l,
    reward_hbm, grad_in_hbm, grad_out_hbm, tile_in, tile_out, sem,
):
    copies = [pltpu.make_async_copy(reward, reward_hbm, sem.at[7])]
    copies[0].start()
    for n in range(HS // 256):
        cols = pl.ds(n * 256, 256)
        v = dot_tn(hid_l[0, :, cols], err_l[0]) + dot_tn(hid_l[1, :, cols], err_l[1])
        tile_out[cols, :] = acc_out[cols, :] + v
        copies.append(
            pltpu.make_async_copy(tile_out.at[cols], grad_out_hbm.at[0, cols], sem.at[n])
        )
        copies[-1].start()
    for n in range(FH // 256):
        cols = pl.ds(n * 256, 256)
        v = dot_tn(rows_l[0, :, cols], pre_l[0]) + dot_tn(rows_l[1, :, cols], pre_l[1])
        tile_in[cols, :] = acc_in[cols, :] + v
        copies.append(
            pltpu.make_async_copy(tile_in.at[cols], grad_in_hbm.at[0, cols], sem.at[4 + n])
        )
        copies[-1].start()
    for copy in copies:
        copy.wait()


def per_device(rows_in, target, w_in, w_out):
    any_spec = pl.BlockSpec(memory_space=pl.ANY)
    vmem_spec = pl.BlockSpec(memory_space=pltpu.VMEM)
    vmem = pltpu.VMEM
    dma = pltpu.SemaphoreType.DMA
    parts = pl.pallas_call(
        kernel,
        out_shape=(
            vmem((1, 16), F32),
            vmem((FH, HS), F32),
            vmem((HS, FH), F32),
            vmem((2, LN, HS), BF16),
            vmem((2, LN, HS), BF16),
            vmem((2, LN, FH), BF16),
            vmem((2, LN, FH), BF16),
        ),
        in_specs=[any_spec] * 4,
        out_specs=(vmem_spec,) * 7,
        scratch_shapes=[
            vmem((F, HS), BF16),
            vmem((HS, F), BF16),
            vmem((R, F), BF16),
            vmem((R, FQ), BF16),
            vmem((LB, FH), BF16),
            vmem((2, LB, HS), BF16),
            vmem((R, HS), F32),
            vmem((4, R, FQ), F32),
            vmem((3, 2, R // 2, FQ), BF16),
            vmem((3, 2, R // 2, FQ), BF16),
            vmem((R, F), BF16),
            vmem((LB, FH), BF16),
            vmem((2, LB, HS), BF16),
            vmem((R, FQ), BF16),
            vmem((MEMBERS, 64, FQ), BF16),
            vmem((64, 128), F32),
            vmem((3, 16, 128), F32),
            dma((4,)),
            dma((3,)),
            dma((3,)),
            dma((len(HOPS),)),
            dma((len(HOPS),)),
            dma((NC, 3, 2)),
            dma((NC, 3, 2)),
            dma((NC, 3, 2)),
            dma((NC, 3, 2)),
            dma((2, NC)),
            dma((2, NC)),
            dma((2, NG)),
            dma((2, NG)),
            dma((len(STRIPS),)),
            dma((MEMBERS, 2)),
            dma((2,)),
            dma((3,)),
            dma((3,)),
        ],
        compiler_params=pltpu.CompilerParams(
            collective_id=0, has_side_effects=True, vmem_limit_bytes=46 * 1024 * 1024
        ),
        name="ensemble",
    )(rows_in, target, w_in, w_out)
    reward, grad_in, grad_out = pl.pallas_call(
        finish,
        out_shape=(
            jax.ShapeDtypeStruct((1, 16), F32),
            jax.ShapeDtypeStruct((1, FH, HS), F32),
            jax.ShapeDtypeStruct((1, HS, FH), F32),
        ),
        in_specs=[vmem_spec] * 7,
        out_specs=(any_spec,) * 3,
        scratch_shapes=[vmem((FH, HS), F32), vmem((HS, FH), F32), dma((8,))],
        compiler_params=pltpu.CompilerParams(vmem_limit_bytes=24 * 1024 * 1024),
        name="finish",
    )(*parts)
    return reward.reshape(16), grad_in, grad_out


def solution(mesh):
    return jax.shard_map(
        per_device,
        mesh=mesh,
        in_specs=(
            P(("batch", "member", "tensor"), None),
            P(("batch", "member"), "tensor"),
            P("member", None, "tensor"),
            P("member", "tensor", None),
        ),
        out_specs=(
            P(("batch", "member", "tensor")),
            P("member", "batch", "tensor"),
            P("member", "tensor", "batch"),
        ),
        check_vma=False,
    )
```

```python
import jax
import jax.numpy as jnp
from jax import lax
from jax.experimental import pallas as pl
from jax.experimental.pallas import tpu as pltpu
from jax.sharding import PartitionSpec as P

MESH = pl.DeviceIdType.MESH
F32 = jnp.float32
BF16 = jnp.bfloat16

F = 1536
FH = F // 2
FQ = F // 4
HS = 1024
R = 1024
ST = 32
MEMBERS = 16
SCALE = 2048.0**-0.5

CHUNKS = (
    ("A00", "B00"),
    ("A01", "A03", "B10", "B30"),
    ("A10", "A30", "B01", "B03"),
    ("A11", "A13", "A31", "A33", "B11", "B31", "B13", "B33"),
    ("A02", "A12", "A32", "B20", "B21", "B23"),
    ("A20", "A23", "B02", "B32"),
    ("A21", "A22", "B12", "B22"),
)
STRIPS = tuple(s for chunk in CHUNKS for s in chunk)
POS = {s: ST * k for k, s in enumerate(STRIPS)}
SIZE = tuple(ST * len(chunk) for chunk in CHUNKS)
OFF = tuple(sum(SIZE[:c]) for c in range(len(CHUNKS)))
NC = len(CHUNKS)
GROUPS = ((0, 1, 2), (3,), (4,), (5, 6))
NG = len(GROUPS)
LAST = GROUPS[-1]
LB = OFF[LAST[0]]
LN = R - LB

HOPS = (
    ("p1", "A00", 0, 32, "A03", (0, 1)),
    ("p1", "A00", 0, 32, "A01", (0, 3)),
    ("p1", "B00", 0, 32, "B30", (1, 0)),
    ("p1", "B00", 0, 32, "B10", (3, 0)),
    ("p2", "A00", 0, 32, "A30", (1, 0)),
    ("p2", "A00", 0, 32, "A10", (3, 0)),
    ("p2", "B00", 0, 32, "B03", (0, 1)),
    ("p2", "B00", 0, 32, "B01", (0, 3)),
    ("d", "A03", 0, 16, "A02", (0, 1)),
    ("d", "A01", 16, 16, "A02", (0, 3)),
    ("d", "B30", 0, 16, "B20", (1, 0)),
    ("d", "B10", 16, 16, "B20", (3, 0)),
    ("q3", "A01", 0, 64, "A31", (1, 0)),
    ("q3", "A01", 0, 64, "A11", (3, 0)),
    ("q3", "B10", 0, 64, "B13", (0, 1)),
    ("q3", "B10", 0, 64, "B11", (0, 3)),
    ("q4", "A02", 0, 32, "A32", (1, 0)),
    ("q4", "A02", 0, 32, "A12", (3, 0)),
    ("q4", "B20", 0, 32, "B23", (0, 1)),
    ("q4", "B20", 0, 32, "B21", (0, 3)),
    ("q5", "A33", 0, 32, "A23", (1, 0)),
    ("q5", "A10", 0, 32, "A20", (3, 0)),
    ("q5", "B33", 0, 32, "B32", (0, 1)),
    ("q5", "B01", 0, 32, "B02", (0, 3)),
    ("q6", "A32", 0, 32, "A22", (1, 0)),
    ("q6", "A11", 0, 32, "A21", (3, 0)),
    ("q6", "B23", 0, 32, "B22", (0, 1)),
    ("q6", "B11", 0, 32, "B12", (0, 3)),
)
HOPS += tuple((h[0].upper(),) + h[1:] for h in HOPS)
GOALS = ((), ("P1",), ("P2",), ("Q3",), ("D", "Q4"), ("Q5",), ("Q6",))
NEEDS = ((), ("p1",), ("p2",), ("q3",), ("d", "q4"), ("q5",), ("q6",))
RELAY = {
    "X1": (("p1",), ("d", "q3")),
    "X2": (("d",), ("q4",)),
    "X3": (("p2", "q3"), ("q5",)),
    "X4": (("q3", "q4"), ("q6",)),
    "X5": ((), ("P1", "P2")),
    "X6": (("P1",), ("D", "Q3")),
    "X7": (("D", "P2", "Q3"), ("Q4", "Q5")),
    "X8": (("Q4",), ("Q6",)),
}
ORDER = (
    "P1", "F0", "G0", "H0", "R0", "X1", "F1", "G1", "X5", "S0", "F2", "G2", "H2", "H1", "R1",
    "X2", "E0", "R2", "S1", "A0", "F3", "S2", "X3", "G3", "E1", "X6", "F4", "E2", "G4", "H3",
    "F5", "X4", "H5", "H4", "G5", "W0", "W1", "R3", "A2", "X7", "R4", "F6", "A1", "H6", "S3",
    "X8", "G6", "W2", "S4", "R5", "T3", "B0", "E3", "R6", "A3", "W3", "S5", "T3", "I0", "S6",
    "E4", "W4", "O0", "E5", "W5", "E6", "W6", "T3", "B1", "A4", "A5", "O1", "A6", "I1", "T2",
    "B2", "Y1", "B3", "O2", "I2", "Y2", "Z1",
)


def dot(a, b):
    return lax.dot_general(a, b, (((1,), (0,)), ((), ())), preferred_element_type=F32)


def dot_nt(a, b):
    return lax.dot_general(a, b, (((1,), (1,)), ((), ())), preferred_element_type=F32)


def dot_tn(a, b):
    return lax.dot_general(a, b, (((0,), (0,)), ((), ())), preferred_element_type=F32)


def kernel(
    rows_hbm, target_hbm, w_in_hbm, w_out_hbm,
    reward_ref, acc_in, acc_out, hid_l, pre_l, err_l, rows_l,
    w_in, w_out, rows, goal, rows_o, hid, slope, part, sbuf, rbuf, err, err_o, pre,
    pred_b, gathered, spread, spread_r,
    loc_sem, zg_s, zg_r, xy_s, xy_r, rs_s, rs_r, ag_s, ag_r, core_s, core_r, grp_s, grp_r,
    rw_s, rw_r, rwl_sem, rz_s, rz_r,
):
    b = lax.axis_index("batch")
    m = lax.axis_index("member")
    t = lax.axis_index("tensor")
    y, x = m // 4, m % 4

    def z_dev(d):
        return (b, m, (t + d) % 4)

    def plane_dev(dy, dx):
        return (b, ((y + dy) % 4) * 4 + (x + dx) % 4, t)

    other = (1 - b, m, t)

    def remote(src, dst, s, r, dev):
        return pltpu.make_async_remote_copy(
            src_ref=src, dst_ref=dst, send_sem=s, recv_sem=r, device_id=dev, device_id_type=MESH
        )

    started = []

    def go(copy):
        copy.start()
        started.append(copy)

    def al(v, k):
        return pl.multiple_of(v, k)

    def quarter(q):
        return pl.ds(al((q % 4) * FQ, 128), FQ)

    mine_cols = pl.ds(al(b * FH, 128), FH)
    other_cols = pl.ds(al((1 - b) * FH, 128), FH)

    barrier = pltpu.get_barrier_semaphore()
    for d in range(1, 4):
        pl.semaphore_signal(barrier, inc=1, device_id=z_dev(d), device_id_type=MESH)
    pl.semaphore_signal(barrier, inc=1, device_id=other, device_id_type=MESH)

    for dy, dx in ((0, 1), (0, 3), (1, 0), (3, 0)):
        pl.semaphore_signal(barrier, inc=1, device_id=plane_dev(dy, dx), device_id_type=MESH)

    own_rows = rows.at[pl.ds(al(t * 16, 16), 16)]
    load_rows = pltpu.make_async_copy(rows_hbm, own_rows, loc_sem.at[0])
    load_target = pltpu.make_async_copy(
        target_hbm, goal.at[pl.ds(0, 64)], loc_sem.at[1]
    )
    load_w_in = pltpu.make_async_copy(w_in_hbm.at[0], w_in, loc_sem.at[2])
    load_w_out = pltpu.make_async_copy(w_out_hbm.at[0], w_out, loc_sem.at[3])
    load_rows.start()
    load_target.start()
    load_w_in.start()
    load_w_out.start()
    pl.semaphore_wait(barrier, 3 + 1 + 4)

    load_rows.wait()
    for d in (2, 1, 3):
        go(remote(own_rows, own_rows, zg_s.at[d - 1], zg_r.at[d - 1], z_dev(d)))
    for d in (1, 3, 2):
        theirs = rows.at[pl.ds(al(((t + 4 - d) % 4) * 16, 16), 16)]
        remote(own_rows, theirs, zg_s.at[d - 1], zg_r.at[d - 1], z_dev(d)).wait_recv()

    def hop(k):
        name, first, skip, n, land, (dy, dx) = HOPS[k]
        of = goal if name.isupper() else rows
        return remote(
            of.at[pl.ds(POS[first] + skip, n)],
            of.at[pl.ds(POS[land] + skip, n)],
            xy_s.at[k],
            xy_r.at[k],
            plane_dev(dy, dx),
        )

    here = set()

    def arrived(names):
        for name in names:
            if name not in here:
                here.add(name)
                for k in range(len(HOPS)):
                    if HOPS[k][0] == name:
                        hop(k).wait_recv()

    def send_hops(names):
        for name in names:
            for k in range(len(HOPS)):
                if HOPS[k][0] == name:
                    go(hop(k))

    def hid_of(whose, c):
        if c in LAST:
            return hid_l.at[whose, pl.ds(OFF[c] - LB, SIZE[c])]
        return hid.at[whose, pl.ds(OFF[c], SIZE[c])]

    def core_copy(kind, c):
        r = pl.ds(OFF[c], SIZE[c])
        if kind == 1:
            src, dst = hid_of(0, c), hid_of(1, c)
        elif c in LAST:
            src, dst = rows.at[r, other_cols], rows_l.at[1, pl.ds(OFF[c] - LB, SIZE[c])]
        else:
            src, dst = rows.at[r, other_cols], rows_o.at[r]
        return remote(src, dst, core_s.at[kind, c], core_r.at[kind, c], other)

    def forward(c):
        arrived(NEEDS[c])
        if c == 0:
            load_w_in.wait()
        r = pl.ds(OFF[c], SIZE[c])
        go(core_copy(0, c))
        out = hid_of(0, c)

        @pl.loop(0, HS // 256, unroll=True)
        def _(n):
            cols = pl.ds(al(n * 256, 256), 256)
            v = dot(rows[r], w_in[:, cols])
            s = jax.nn.sigmoid(v)
            out[:, cols] = (v * s).astype(BF16)
            slope[r, cols] = s * (1.0 + v * (1.0 - s))

        go(core_copy(1, c))

    def halves(c, way):
        h = SIZE[c] // 2
        return pl.ds(OFF[c] + way * h, h), pl.ds(OFF[c] // 2, h)

    def predict(c, rel):
        r = pl.ds(OFF[c], SIZE[c])
        part[rel, r] = dot(hid_of(0, c)[...], w_out[:, quarter(t + rel)])

    def predict_first(c):
        if c == 0:
            load_w_out.wait()
        for way, rel in ((0, 3), (1, 1)):
            predict(c, rel)
            r, q = halves(c, way)
            sbuf[0, way, q] = part[rel, r].astype(BF16)
            go(rs(c, 0, way))

    def rs(c, s, way):
        _, q = halves(c, way)
        return remote(
            sbuf.at[s, way, q], rbuf.at[s, way, q], rs_s.at[c, s, way], rs_r.at[c, s, way],
            z_dev(1 + 2 * way),
        )

    def rs_step(c, s):
        for way in range(2):
            rs(c, s - 1, way).wait_recv()
            rel = (3 - s) if way == 0 else (1 + s)
            r, q = halves(c, way)
            sbuf[s, way, q] = (part[rel, r] + rbuf[s - 1, way, q].astype(F32)).astype(BF16)
            go(rs(c, s, way))

    def ag_copy(c, k, way, incoming):
        r, _ = halves(c, way if k != 1 else 1 - way)
        source = t if k < 2 else t + 3 - 2 * way
        if incoming:
            source = source + 3 - 2 * way
        ref = err.at[r, quarter(source)]
        return remote(ref, ref, ag_s.at[c, k, way], ag_r.at[c, k, way], z_dev(1 + 2 * way))

    def errors(c):
        arrived(GOALS[c])
        for way in range(2):
            rs(c, 2, way).wait_recv()
            r, q = halves(c, way)
            pred = part[0, r] + rbuf[2, way, q].astype(F32)
            err[r, quarter(t)] = ((pred - goal[r].astype(F32)) * SCALE).astype(BF16)
            pred_b[r] = pred.astype(BF16)
            go(ag_copy(c, 0, way, False))
        for way in range(2):
            go(ag_copy(c, 1, way, False))

    def ag_forward(c):
        for way in range(2):
            ag_copy(c, 0, way, True).wait_recv()
            go(ag_copy(c, 2, way, False))

    def reward_send(c):
        for strip in CHUNKS[c]:
            half, dy, dx = int(strip[0] == "B"), int(strip[1]), int(strip[2])
            k = POS[strip] // ST
            src = pred_b.at[pl.ds(POS[strip], ST)]
            dst = gathered.at[m, pl.ds(ST * half, ST)]
            if (dy, dx) == (0, 0):
                pltpu.make_async_copy(src, dst, rwl_sem.at[half]).start()
            else:
                go(remote(src, dst, rw_s.at[k], rw_r.at[m, half], plane_dev(dy, dx)))

    def group_rows(g):
        c0, c1 = GROUPS[g][0], GROUPS[g][-1]
        return pl.ds(OFF[c0], OFF[c1] + SIZE[c1] - OFF[c0])

    def group_copy(kind, g):
        r = group_rows(g)
        last = g == NG - 1
        if kind == 0:
            src, dst = err.at[r, other_cols], err_l.at[1] if last else err_o.at[r]
        elif last:
            src, dst = pre_l.at[0], pre_l.at[1]
        else:
            src, dst = pre.at[0, r], pre.at[1, r]
        return remote(src, dst, grp_s.at[kind, g], grp_r.at[kind, g], other)

    def back(g):
        for c in GROUPS[g]:
            for k in (1, 2):
                for way in range(2):
                    ag_copy(c, k, way, True).wait_recv()
        go(group_copy(0, g))
        r = group_rows(g)
        out = pre_l.at[0] if g == NG - 1 else pre.at[0, r]

        @pl.loop(0, HS // 256, unroll=True)
        def _(n):
            cols = pl.ds(al(n * 256, 256), 256)
            v = dot_nt(err[r], w_out[cols, :])
            out[:, cols] = (v * slope[r, cols]).astype(BF16)

        go(group_copy(1, g))
        if g == NG - 1:
            err_l[0] = err[r, mine_cols]
            rows_l[0] = rows[r, mine_cols]

    def last_arrived():
        for c in LAST:
            core_copy(0, c).wait_recv()
            core_copy(1, c).wait_recv()
        group_copy(0, NG - 1).wait_recv()
        group_copy(1, NG - 1).wait_recv()

    begun = set()

    def grad_out(g):
        for c in GROUPS[g]:
            core_copy(1, c).wait_recv()
        group_copy(0, g).wait_recv()
        r = group_rows(g)
        first = "out" not in begun
        begun.add("out")

        @pl.loop(0, HS // 256, unroll=True)
        def _(n):
            cols = pl.ds(al(n * 256, 256), 256)
            v = dot_tn(hid[0, r, cols], err[r, mine_cols]) + dot_tn(hid[1, r, cols], err_o[r])
            acc_out[cols, :] = v if first else acc_out[cols, :] + v

    def grad_in(g):
        for c in GROUPS[g]:
            core_copy(0, c).wait_recv()
        group_copy(1, g).wait_recv()
        r = group_rows(g)
        first = "in" not in begun
        begun.add("in")

        @pl.loop(0, FH // 256, unroll=True)
        def _(n):
            mine = pl.ds(al(b * FH + n * 256, 128), 256)
            cols = pl.ds(al(n * 256, 256), 256)
            v = dot_tn(rows[r, mine], pre[0, r]) + dot_tn(rows_o[r, cols], pre[1, r])
            acc_in[cols, :] = v if first else acc_in[cols, :] + v

    def spread_copy(d):
        return remote(
            spread.at[pl.ds(al(((t + d) % 4) * 16, 16), 16)],
            spread_r.at[d - 1],
            rz_s.at[d - 1],
            rz_r.at[d - 1],
            z_dev(d),
        )

    def reward_first():
        @pl.loop(1, MEMBERS)
        def _(d):
            s = (m + d) % MEMBERS
            for half in range(2):
                remote(
                    pred_b.at[pl.ds(0, ST)],
                    gathered.at[s, pl.ds(ST * half, ST)],
                    rw_s.at[2],
                    rw_r.at[s, half],
                    (b, s, t),
                ).wait_recv()

        for half in range(2):
            pltpu.make_async_copy(
                pred_b.at[pl.ds(ST * half, ST)],
                gathered.at[m, pl.ds(ST * half, ST)],
                rwl_sem.at[half],
            ).wait()

        total = jnp.zeros((64, 128), F32)
        for k in range(3):
            cols = pl.ds(128 * k, 128)
            mean = jnp.zeros((64, 128), F32)
            for s in range(MEMBERS):
                mean += gathered[s, :, cols].astype(F32)
            mean = mean * (1.0 / MEMBERS)
            for s in range(MEMBERS):
                dev = gathered[s, :, cols].astype(F32) - mean
                total += dev * dev
        spread[...] = total
        for d in range(1, 4):
            go(spread_copy(d))

    def reward_last():
        for d in range(1, 4):
            spread_copy(d).wait_recv()
        own = spread[pl.ds(al(t * 16, 16), 16)]
        for d in range(3):
            own += spread_r[d]
        reward_ref[...] = jnp.sum(own.T, axis=0, keepdims=True) * (1.0 / (MEMBERS * F))

    def sent(keep):
        while len(started) > keep:
            started.pop(0).wait_send()

    for step in ORDER:
        kind, k = step[0], int(step[1:])
        if kind == "P":
            send_hops(("p1", "p2"))
        elif kind == "X":
            if step == "X5":
                load_target.wait()
            arrived(RELAY[step][0])
            send_hops(RELAY[step][1])
        elif kind == "F":
            forward(k)
        elif kind == "G":
            predict_first(k)
        elif kind == "H":
            predict(k, 2)
            predict(k, 0)
        elif kind == "R":
            rs_step(k, 1)
        elif kind == "S":
            rs_step(k, 2)
        elif kind == "E":
            errors(k)
        elif kind == "A":
            ag_forward(k)
        elif kind == "W":
            reward_send(k)
        elif kind == "B":
            back(k)
        elif kind == "O":
            grad_out(k)
        elif kind == "I":
            grad_in(k)
        elif kind == "T":
            sent(10 * k)
        elif kind == "Z":
            last_arrived()
        elif step == "Y1":
            reward_first()
        else:
            reward_last()
    sent(0)


def finish(
    reward, acc_in, acc_out, hid_l, pre_l, err_l, rows_l,
    reward_hbm, grad_in_hbm, grad_out_hbm, tile_in, tile_out, sem,
):
    copies = [pltpu.make_async_copy(reward, reward_hbm, sem.at[7])]
    copies[0].start()
    for n in range(HS // 256):
        cols = pl.ds(n * 256, 256)
        v = dot_tn(hid_l[0, :, cols], err_l[0]) + dot_tn(hid_l[1, :, cols], err_l[1])
        tile_out[cols, :] = acc_out[cols, :] + v
        copies.append(
            pltpu.make_async_copy(tile_out.at[cols], grad_out_hbm.at[0, cols], sem.at[n])
        )
        copies[-1].start()
    for n in range(FH // 256):
        cols = pl.ds(n * 256, 256)
        v = dot_tn(rows_l[0, :, cols], pre_l[0]) + dot_tn(rows_l[1, :, cols], pre_l[1])
        tile_in[cols, :] = acc_in[cols, :] + v
        copies.append(
            pltpu.make_async_copy(tile_in.at[cols], grad_in_hbm.at[0, cols], sem.at[4 + n])
        )
        copies[-1].start()
    for copy in copies:
        copy.wait()


def per_device(rows_in, target, w_in, w_out):
    any_spec = pl.BlockSpec(memory_space=pl.ANY)
    vmem_spec = pl.BlockSpec(memory_space=pltpu.VMEM)
    vmem = pltpu.VMEM
    dma = pltpu.SemaphoreType.DMA
    parts = pl.pallas_call(
        kernel,
        out_shape=(
            vmem((1, 16), F32),
            vmem((FH, HS), F32),
            vmem((HS, FH), F32),
            vmem((2, LN, HS), BF16),
            vmem((2, LN, HS), BF16),
            vmem((2, LN, FH), BF16),
            vmem((2, LN, FH), BF16),
        ),
        in_specs=[any_spec] * 4,
        out_specs=(vmem_spec,) * 7,
        scratch_shapes=[
            vmem((F, HS), BF16),
            vmem((HS, F), BF16),
            vmem((R, F), BF16),
            vmem((R, FQ), BF16),
            vmem((LB, FH), BF16),
            vmem((2, LB, HS), BF16),
            vmem((R, HS), F32),
            vmem((4, R, FQ), F32),
            vmem((3, 2, R // 2, FQ), BF16),
            vmem((3, 2, R // 2, FQ), BF16),
            vmem((R, F), BF16),
            vmem((LB, FH), BF16),
            vmem((2, LB, HS), BF16),
            vmem((R, FQ), BF16),
            vmem((MEMBERS, 64, FQ), BF16),
            vmem((64, 128), F32),
            vmem((3, 16, 128), F32),
            dma((4,)),
            dma((3,)),
            dma((3,)),
            dma((len(HOPS),)),
            dma((len(HOPS),)),
            dma((NC, 3, 2)),
            dma((NC, 3, 2)),
            dma((NC, 3, 2)),
            dma((NC, 3, 2)),
            dma((2, NC)),
            dma((2, NC)),
            dma((2, NG)),
            dma((2, NG)),
            dma((len(STRIPS),)),
            dma((MEMBERS, 2)),
            dma((2,)),
            dma((3,)),
            dma((3,)),
        ],
        compiler_params=pltpu.CompilerParams(
            collective_id=0, has_side_effects=True, vmem_limit_bytes=46 * 1024 * 1024
        ),
        name="ensemble",
    )(rows_in, target, w_in, w_out)
    reward, grad_in, grad_out = pl.pallas_call(
        finish,
        out_shape=(
            jax.ShapeDtypeStruct((1, 16), F32),
            jax.ShapeDtypeStruct((1, FH, HS), F32),
            jax.ShapeDtypeStruct((1, HS, FH), F32),
        ),
        in_specs=[vmem_spec] * 7,
        out_specs=(any_spec,) * 3,
        scratch_shapes=[vmem((FH, HS), F32), vmem((HS, FH), F32), dma((8,))],
        compiler_params=pltpu.CompilerParams(vmem_limit_bytes=24 * 1024 * 1024),
        name="finish",
    )(*parts)
    return reward.reshape(16), grad_in, grad_out


def solution(mesh):
    return jax.shard_map(
        per_device,
        mesh=mesh,
        in_specs=(
            P(("batch", "member", "tensor"), None),
            P(("batch", "member"), "tensor"),
            P("member", None, "tensor"),
            P("member", "tensor", None),
        ),
        out_specs=(
            P(("batch", "member", "tensor")),
            P("member", "batch", "tensor"),
            P("member", "tensor", "batch"),
        ),
        check_vma=False,
    )
```
